32 devices in a mesh: user: 2 (over x), item: 16 (over z, y, core).
Axes of the slice: x: 2, y: 2, z: 4, core: 2. Of those that a mesh axis runs over, the one named last changes fastest.
Arguments:
- play_counts: int32 [16, 62, 96, 512], P('item', 'user'), may hold values from 0 to 4096
- tile_owner: int32 [16, 62], P('item', 'user'), may hold values from 0 to 1, as said below
- tile_cell: int32 [16, 62], P('item', 'user'), may hold values from 0 to 31, as said below
- tile_rows: int32 [16, 62], P('item', 'user'), may hold values from 48 to 96
- tile_cols: int32 [16, 62], P('item', 'user'), may hold values from 256 to 512
- item_factors: bfloat16 [32768, 256], P('item')
Outputs:
- folded: float32 [1536, 256], P('user', 'item')
The draws below stay inside these ranges and needn't reach their ends.
Inputs may be any that keep to these rules, and one draw needn't show every extreme that they name: `tile_owner`: for each item shard, an ingest position sends at most 16 tiles to one owner, and some owner gets exactly 16 of them. `tile_cell`: among the tiles of one item shard bound for one owner, no two share a cell.
All inputs are finite; a program needn't handle non-finite values.
Results may differ from the reference program's by a relative error of at most 0.0039.
Values may be sent and summed in bfloat16 or wider, within the bound.
No kernel may reach another device: no remote copies, remote signals or barrier semaphores. Data moves between devices by JAX's collectives and lax.ppermute only.
A program may use at most 64 MiB of HBM per device.

```python
import math
import jax
import jax.numpy as jnp
from jax import lax

K = 256
TR = 96
TC = 512
GROUPS = 8
CBLK = 4
ITERS = 4
CELLS = 32
CAP = 16
TILES_DEV = 31
ITEMS = 32768
N_USER = 2
N_ITEM = 16


def routing(key):

    def one_shard(shard_key):
        key_owner, key_cell = jax.random.split(shard_key)
        base = jnp.repeat(jnp.arange(N_USER, dtype=jnp.int32), CAP)
        owner_keys = jax.random.split(key_owner, N_USER)
        owners = jax.vmap(lambda single: jax.random.permutation(single, base)[:TILES_DEV])(owner_keys)
        flat = owners.reshape(-1)
        onehot = (flat[:, None] == jnp.arange(N_USER, dtype=jnp.int32)[None, :]).astype(jnp.int32)
        ranking = jnp.sum((jnp.cumsum(onehot, axis=0) - onehot) * onehot, axis=1)
        cell_keys = jax.random.split(key_cell, N_USER)
        orders = jax.vmap(lambda single: jax.random.permutation(single, CELLS))(cell_keys)
        cells = orders[flat, ranking].astype(jnp.int32)
        return (flat, cells)
    owners, cells = jax.vmap(one_shard)(jax.random.split(jax.random.fold_in(key, 17), N_ITEM))
    return (owners, cells)


def draw_tile_owner(key, part):
    return routing(key)[0]


def draw_tile_cell(key, part):
    return routing(key)[1]


def draw_play_counts(key, part):
    key_hit, key_expo, key_value = jax.random.split(jax.random.fold_in(key, 5), 3)
    shape = (N_ITEM, N_USER * TILES_DEV, TR, TC)
    level = 200 + 400 * jnp.arange(N_ITEM, dtype=jnp.int32) // max(N_ITEM - 1, 1)
    hit = jax.random.randint(key_hit, shape, 0, 1000) < level[:, None, None, None]
    expo = jax.random.randint(key_expo, shape, 1, 13)
    raw = jax.random.randint(key_value, shape, 0, 4096)
    value = 1 + jnp.remainder(raw, jnp.left_shift(jnp.int32(1), expo))
    return jnp.where(hit, value, 0).astype(jnp.int32)


def draw_item_factors(key, part):
    key_col, key_row, key_base = jax.random.split(jax.random.fold_in(key, 3), 3)
    column_scale = jnp.exp(jax.random.uniform(key_col, (K,), jnp.float32, math.log(0.25), math.log(2.5)))
    row_scale = jnp.exp(jax.random.uniform(key_row, (ITEMS, 1), jnp.float32, math.log(0.5), math.log(2.0)))
    base = jax.random.normal(key_base, (ITEMS, K), jnp.float32)
    return (base * row_scale * column_scale[None, :] / math.sqrt(ITEMS)).astype(jnp.bfloat16)


def touch_ends(entries, rng, low, top_value):
    spot = [jax.random.randint(jax.random.fold_in(rng, axis), (), 0, length) for axis, length in enumerate(entries.shape)]
    main_axis = entries.shape.index(max(entries.shape))
    beside = spot[:main_axis] + [(spot[main_axis] + 1) % entries.shape[main_axis]] + spot[main_axis + 1:]
    return entries.at[tuple(spot)].set(low).at[tuple(beside)].set(top_value)


def setup_inputs(seed: int = 0) -> dict:
    keys = jax.random.split(jax.random.key(seed), 7)
    return {
        "play_counts": draw_play_counts(jax.random.fold_in(keys[6], 71), 0),
        "tile_owner": draw_tile_owner(jax.random.fold_in(keys[6], 71), 0),
        "tile_cell": draw_tile_cell(jax.random.fold_in(keys[6], 71), 0),
        "tile_rows": touch_ends(jax.random.randint(keys[3], (N_ITEM, N_USER * TILES_DEV), TR // 2, TR + 1), jax.random.fold_in(keys[3], 1), TR // 2, TR).astype(jnp.int32),
        "tile_cols": touch_ends(jax.random.randint(keys[4], (N_ITEM, N_USER * TILES_DEV), TC // 2, TC + 1), jax.random.fold_in(keys[4], 1), TC // 2, TC).astype(jnp.int32),
        "item_factors": draw_item_factors(jax.random.fold_in(keys[6], 71), 0),
    }


EPS = 1.0
GUARD = 1e-6


def tile_weights(counts, rows, cols):
    rank_rows = lax.broadcasted_iota(jnp.int32, counts.shape, counts.ndim - 2)
    rank_cols = lax.broadcasted_iota(jnp.int32, counts.shape, counts.ndim - 1)
    inside = (rank_rows < rows[..., None, None]) & (rank_cols < cols[..., None, None])
    values = jnp.log1p(counts.astype(jnp.float32) / EPS)
    return jnp.where(inside, values, jnp.float32(0.0)).astype(jnp.bfloat16)


def fold_block(plays, factors, n_items):
    confidence = 1.0 + plays.astype(jnp.float32)
    observed = plays > 0
    weighted = jnp.where(observed, confidence, jnp.float32(0.0)).astype(jnp.bfloat16)
    seen = jnp.sum(observed.astype(jnp.float32), axis=1)
    reg = seen / n_items

    def apply(vector):
        projected = lax.dot_general(vector.astype(jnp.bfloat16), factors, (((1,), (1,)), ((), ())), preferred_element_type=jnp.float32)
        scaled = (confidence * projected).astype(jnp.bfloat16)
        return jnp.dot(scaled, factors, preferred_element_type=jnp.float32) + reg[:, None] * vector

    rhs = jnp.dot(weighted, factors, preferred_element_type=jnp.float32)
    folded = jnp.zeros_like(rhs)
    residual = rhs
    direction = rhs
    norm_now = jnp.sum(residual * residual, axis=1)
    for number in range(ITERS):
        image = apply(direction)
        alpha = norm_now / (jnp.sum(direction * image, axis=1) + GUARD)
        folded = folded + alpha[:, None] * direction
        residual = residual - alpha[:, None] * image
        fresh = jnp.sum(residual * residual, axis=1)
        direction = residual + (fresh / (norm_now + GUARD))[:, None] * direction
        norm_now = fresh
    return folded


def reference(play_counts, tile_owner, tile_cell, tile_rows, tile_cols, item_factors):
    cells_all = GROUPS * CBLK

    def owner_block(owner):
        def shard(index):
            weights = tile_weights(play_counts[index], tile_rows[index], tile_cols[index]).reshape(-1, TR * TC)
            place = ((tile_owner[index] == owner)[None, :] & (tile_cell[index][None, :] == jnp.arange(cells_all, dtype=jnp.int32)[:, None])).astype(jnp.float32)
            return jnp.dot(place, weights.astype(jnp.float32), precision=lax.Precision.HIGHEST).astype(jnp.bfloat16)

        grids = lax.map(shard, jnp.arange(N_ITEM, dtype=jnp.int32))
        plays = grids.reshape(N_ITEM, GROUPS, CBLK, TR, TC).transpose(1, 3, 0, 2, 4).reshape(GROUPS * TR, N_ITEM * CBLK * TC)
        return fold_block(plays, item_factors, float(ITEMS))

    blocks = lax.map(owner_block, jnp.arange(N_USER, dtype=jnp.int32))
    return blocks.reshape(N_USER * GROUPS * TR, item_factors.shape[1])
```

```python
import functools

import jax
import jax.numpy as jnp
from jax import lax
from jax.experimental import pallas as pl
from jax.experimental.pallas import tpu as pltpu
from jax.sharding import PartitionSpec as P

GROUPS = 8
CBLK = 4
ITERS = 4

EPS = 1.0
GUARD = 1e-06

HALVES = 2
HG = GROUPS // HALVES

BF16 = jnp.bfloat16
F32 = jnp.float32
VMEM = pl.BlockSpec(memory_space=pltpu.VMEM)
SMEM = pl.BlockSpec(memory_space=pltpu.SMEM)
ANY = pl.BlockSpec(memory_space=pl.ANY)


def log_tile(counts, rows, cols):
    rank_rows = lax.broadcasted_iota(jnp.int32, counts.shape, 0)
    rank_cols = lax.broadcasted_iota(jnp.int32, counts.shape, 1)
    inside = (rank_rows < rows) & (rank_cols < cols)
    values = jnp.log(1.0 + counts.astype(F32) / EPS)
    return jnp.where(inside, values, 0.0).astype(BF16)


def start_tiles(n_user, cap, own, at, owner, cell, counts, label, slots, fill, buf, sems):
    total = label.shape[0]
    for s in range(total):
        label[s] = -1
        slots[s] = -1
    for s in range(n_user):
        fill[s] = 0

    def visit(t, carry):
        shift = lax.rem(owner[t] - at[0] + n_user, n_user)

        @pl.when((shift == 0) if own else (shift != 0))
        def _():
            base = 0 if own else shift - 1
            k = fill[base]
            slot = base * cap + k
            fill[base] = k + 1
            slots[slot] = t
            label[slot] = cell[t]
            pltpu.make_async_copy(counts.at[t], buf.at[slot], sems.at[slot]).start()

        return carry

    lax.fori_loop(0, counts.shape[0], visit, 0)


def pack_kernel(n_user, cap, at, owner, cell, rows, cols, counts, tiles, label, slots, fill, buf, sems):
    start_tiles(n_user, cap, False, at, owner, cell, counts, label, slots, fill, buf, sems)

    def work(s, carry):
        t = slots[s]

        @pl.when(t >= 0)
        def _():
            pltpu.make_async_copy(counts.at[t], buf.at[s], sems.at[s]).wait()
            tiles[s] = log_tile(buf[s], rows[t], cols[t])

        return carry

    lax.fori_loop(0, tiles.shape[0], work, 0)


def rhs_kernel(
    n_user, cap, at, owner, cell, rows, cols, out_label, counts, out_tiles, factors,
    keep, send, tiles, label, slots, fill, buf, obuf, dense, sems, osem,
):
    start_tiles(n_user, cap, True, at, owner, cell, counts, label, slots, fill, buf, sems)
    moved = pltpu.make_async_copy(out_tiles, obuf, osem)
    moved.start()
    height, width = counts.shape[1], counts.shape[2]
    half = HG * height
    dense[...] = jnp.zeros_like(dense)

    def put(tile, shift, where):
        group, block = where // CBLK, where % CBLK
        side = jnp.where(group // HG == at[1], 0, 1)
        row = side * (n_user * half) + shift * half + (group % HG) * height
        value = tile.astype(F32)
        weighted = jnp.where(value > 0, 1.0 + value, 0.0).astype(BF16)
        dense[pl.ds(pl.multiple_of(row, 16), height), pl.ds(pl.multiple_of(block * width, 128), width)] = weighted

    moved.wait()

    def work_out(s, carry):
        @pl.when(out_label[s] >= 0)
        def _():
            put(obuf[s], s // cap + 1, out_label[s])

        return carry

    lax.fori_loop(0, out_label.shape[0], work_out, 0)

    def work_own(s, carry):
        t = slots[s]

        @pl.when(t >= 0)
        def _():
            pltpu.make_async_copy(counts.at[t], buf.at[s], sems.at[s]).wait()
            tile = log_tile(buf[s], rows[t], cols[t])
            tiles[s] = tile
            put(tile, 0, label[s])

        return carry

    lax.fori_loop(0, cap, work_own, 0)

    def dots(s, carry):
        row = pl.multiple_of(s * half, 16)
        send[pl.ds(row, half), :] = jnp.dot(
            dense[pl.ds(pl.multiple_of((n_user + s) * half, 16), half), :], factors[...], preferred_element_type=F32
        )
        keep[pl.ds(row, half), :] = jnp.dot(dense[pl.ds(row, half), :], factors[...], preferred_element_type=F32)
        return carry

    lax.fori_loop(0, n_user, dots, 0)


def scaled_block(direction, factors, plays):
    projected = lax.dot_general(direction, factors, (((1,), (1,)), ((), ())), preferred_element_type=F32)
    confidence = 1.0 + plays
    return projected, (confidence * projected).astype(BF16)


def lanes(x):
    return sum(x[:, k * 128 : (k + 1) * 128] for k in range(x.shape[1] // 128))


def first_kernel(
    cap, n_items, table, direction, own, far, pair_own, pair_far, factors,
    image, plays, reg, fbuf, seen, acc, sems, fsems,
):
    blocks, half, width = plays.shape
    height = half // HG

    def each(j, act_copy, act_none):
        for g in range(HG):
            code = table[(j // CBLK) * (HG * CBLK) + g * CBLK + j % CBLK]
            near, other = (own, far) if j < CBLK else (pair_own, pair_far)
            target = plays.at[j, g * height : (g + 1) * height, :]
            sem = sems.at[j * HG + g]

            @pl.when((code >= 0) & (code < cap))
            def _(code=code, near=near, target=target, sem=sem):
                act_copy(pltpu.make_async_copy(near.at[code], target, sem))

            @pl.when(code >= cap)
            def _(code=code, other=other, target=target, sem=sem):
                act_copy(pltpu.make_async_copy(other.at[code - cap], target, sem))

            if act_none:

                @pl.when(code < 0)
                def _(target=target):
                    target[...] = jnp.zeros(target.shape, target.dtype)

    def fcopy(j):
        rows = pl.ds(j * width, width)
        return pltpu.make_async_copy(factors.at[rows], fbuf.at[rows], fsems.at[j])

    for j in range(blocks):
        fcopy(j).start()
        each(j, lambda c: c.start(), True)
    for j in range(blocks):
        fcopy(j).wait()
        each(j, lambda c: c.wait(), False)
        block = fbuf[j * width : (j + 1) * width, :]
        value = plays[j].astype(F32)
        _, scaled = scaled_block(direction[...], block, value)
        part = jnp.dot(scaled, block, preferred_element_type=F32)
        count = lanes(jnp.where(value > 0, 1.0, 0.0))
        if j == 0:
            acc[...] = part
            seen[...] = count
        else:
            acc[...] += part
            seen[...] += count
    share = jnp.sum(seen[...], axis=1, keepdims=True) / n_items
    reg[...] = jnp.broadcast_to(share, reg.shape)
    image[...] = (acc[...] + share * direction[...].astype(F32)).astype(BF16)


def load_blocks(plays, factors, pbuf, fbuf, sems, fsems):
    blocks, _, width = pbuf.shape

    def pcopy(j):
        return pltpu.make_async_copy(plays.at[j], pbuf.at[j], sems.at[j])

    def fcopy(j):
        rows = pl.ds(j * width, width)
        return pltpu.make_async_copy(factors.at[rows], fbuf.at[rows], fsems.at[j])

    for j in range(blocks):
        fcopy(j).start()
        pcopy(j).start()

    def get(j):
        fcopy(j).wait()
        pcopy(j).wait()
        return pbuf[j].astype(F32), fbuf[j * width : (j + 1) * width, :]

    return get


def mid_kernel(direction, reg, plays, factors, image, pbuf, fbuf, acc, sems, fsems):
    get = load_blocks(plays, factors, pbuf, fbuf, sems, fsems)
    for j in range(pbuf.shape[0]):
        value, block = get(j)
        _, scaled = scaled_block(direction[...], block, value)
        part = jnp.dot(scaled, block, preferred_element_type=F32)
        if j == 0:
            acc[...] = part
        else:
            acc[...] += part
    image[...] = (acc[...] + reg[:, :1] * direction[...].astype(F32)).astype(BF16)


def last_kernel(direction, reg, base, plays, factors, payload, pbuf, fbuf, acc, sems, fsems):
    get = load_blocks(plays, factors, pbuf, fbuf, sems, fsems)
    for j in range(pbuf.shape[0]):
        value, block = get(j)
        projected, scaled = scaled_block(direction[...], block, value)
        part = lanes(scaled.astype(F32) * projected)
        if j == 0:
            acc[...] = part
        else:
            acc[...] += part
    wide = direction[...].astype(F32)
    along = acc[...] + reg[:, :1] * lanes(wide * wide)
    along = jnp.broadcast_to(jnp.sum(along, axis=1, keepdims=True), acc.shape)
    groups = acc.shape[0] // 8
    first = 128 - payload_lanes(base.shape[0], groups)
    lane = lax.broadcasted_iota(jnp.int32, (8, 128), 1)
    for tile in range(2):
        laid = jnp.zeros((8, 128), F32)
        for g in range(groups):
            if (g >= 128 - first) == tile:
                laid = jnp.where(lane == first + g - tile * (128 - first), along[g * 8 : (g + 1) * 8, :], laid)
        for i in range(base.shape[0]):
            payload[i, tile * 8 : (tile + 1) * 8, :] = base[i, tile * 8 : (tile + 1) * 8, :] + laid


def payload_lanes(n_item, groups):
    return 128 - (groups // (n_item // HALVES)) * (256 // n_item)


def base_kernel(folded, direction, residual, base):
    n_item = base.shape[0]
    rows, rank = folded.shape
    share = rank // n_item
    pieces = rows // 8
    base[...] = jnp.zeros_like(base)
    norm = jnp.sum(residual[...] * residual[...], axis=1, keepdims=True)
    for s in range(pieces):
        at = slice(s * 8, (s + 1) * 8)
        for i in range(n_item):
            base[i, 0:8, s * share : (s + 1) * share] = folded[at, i * share : (i + 1) * share]
            base[i, 8:16, s * share : (s + 1) * share] = direction[at, i * share : (i + 1) * share]
        for i in range(n_item):
            base[i, 8:16, 112 + s : 113 + s] = norm[at, :]


def final_kernel(got, out):
    n_item = got.shape[0]
    n_chunk = n_item // HALVES
    share = out.shape[1]
    half = out.shape[0] // HALVES
    pieces = half // n_chunk // 8
    first = pieces * share
    for h in range(HALVES):
        sums = [sum(got[k * HALVES + h, t * 8 : (t + 1) * 8, :] for k in range(n_chunk)) for t in range(2)]
        for k in range(n_chunk):
            src = k * HALVES + h
            for s in range(pieces):
                g = k * pieces + s
                lane = first + g % (128 - first)
                along = sums[g // (128 - first)][:, lane : lane + 1]
                alpha = got[src, 8:16, 112 + s : 113 + s] / (along + GUARD)
                row = h * half + g * 8
                at = slice(s * share, (s + 1) * share)
                out[row : row + 8, :] = got[src, 0:8, at] + alpha * got[src, 8:16, at]


def vector_kernel(got, direction, residual, folded, direction_out, residual_out, folded_out, spread):
    image = sum(got[k].astype(F32) for k in range(got.shape[0]))
    d, r = direction[...], residual[...]
    norm = jnp.sum(r * r, axis=1, keepdims=True)
    alpha = norm / (jnp.sum(d * image, axis=1, keepdims=True) + GUARD)
    folded_out[...] = folded[...] + alpha * d
    r = r - alpha * image
    fresh = jnp.sum(r * r, axis=1, keepdims=True)
    d = r + fresh / (norm + GUARD) * d
    residual_out[...] = r
    direction_out[...] = d
    low = d.astype(BF16)
    for k in range(spread.shape[0]):
        spread[k] = low


def shards(play_counts, tile_owner, tile_cell, tile_rows, tile_cols, item_factors):
    counts = play_counts[0]
    tiles_dev, height, width = counts.shape
    n_user = lax.axis_size("user")
    n_item = lax.axis_size("item")
    shard_items, rank = item_factors.shape
    cap = GROUPS * CBLK // n_user
    n_out = (n_user - 1) * cap
    n_chunk = n_item // HALVES
    half = HG * height
    chunk = half // n_chunk
    n_items = float(shard_items * n_item)
    blocks = HALVES * CBLK

    user = lax.axis_index("user")
    core = lax.rem(lax.axis_index("item"), HALVES)
    at = jnp.stack([user, core]).astype(jnp.int32)
    pair = [(i, i ^ 1) for i in range(n_item)]
    groups = [[h + HALVES * k for k in range(n_chunk)] for h in range(HALVES)]

    def call(kernel, ins, outs, scratch, flops=0, nbytes=0):
        return pl.pallas_call(
            kernel,
            out_shape=[o[0] for o in outs],
            in_specs=ins,
            out_specs=[o[1] for o in outs],
            scratch_shapes=scratch,
            compiler_params=pltpu.CompilerParams(vmem_limit_bytes=56 * 2**20),
            cost_estimate=pl.CostEstimate(flops=flops, bytes_accessed=nbytes, transcendentals=0),
        )

    def shape(dims, dtype):
        return jax.ShapeDtypeStruct(dims, dtype)

    def over_users(x, shift):
        return lax.ppermute(x, "user", [(u, (u + shift) % n_user) for u in range(n_user)])

    def exchange(x):
        return lax.all_to_all(x, "item", 0, 0, axis_index_groups=groups, tiled=True)

    route = (at, tile_owner[0], tile_cell[0], tile_rows[0], tile_cols[0])
    dma = pltpu.SemaphoreType.DMA
    out_tiles, out_label = call(
        functools.partial(pack_kernel, n_user, cap),
        [SMEM] * 5 + [ANY],
        [(shape((n_out, height, width), BF16), VMEM), (shape((n_out,), jnp.int32), SMEM)],
        [
            pltpu.SMEM((n_out,), jnp.int32),
            pltpu.SMEM((n_user,), jnp.int32),
            pltpu.VMEM((n_out, height, width), jnp.int32),
            dma((n_out,)),
        ],
        nbytes=n_out * height * width * 6,
    )(*route, counts)
    far, far_label = [], []
    for s in range(1, n_user):
        far.append(over_users(out_tiles[(s - 1) * cap : s * cap], s))
        far_label.append(over_users(out_label[(s - 1) * cap : s * cap], s))
    far = jnp.concatenate(far) if n_user > 2 else far[0]
    far_label = jnp.concatenate(far_label) if n_user > 2 else far_label[0]

    keep, send, own, own_label = call(
        functools.partial(rhs_kernel, n_user, cap),
        [SMEM] * 6 + [ANY, ANY, VMEM],
        [
            (shape((n_user * half, rank), F32), VMEM),
            (shape((n_user * half, rank), F32), VMEM),
            (shape((cap, height, width), BF16), VMEM),
            (shape((cap,), jnp.int32), SMEM),
        ],
        [
            pltpu.SMEM((cap,), jnp.int32),
            pltpu.SMEM((n_user,), jnp.int32),
            pltpu.VMEM((cap, height, width), jnp.int32),
            pltpu.VMEM((n_out, height, width), BF16),
            pltpu.VMEM((HALVES * n_user * half, shard_items), BF16),
            dma((cap,)),
            dma(()),
        ],
        flops=2 * HALVES * n_user * half * shard_items * rank,
        nbytes=2 * tiles_dev * height * width * 4,
    )(*route, out_label, counts, out_tiles, item_factors)

    partial_rhs = (keep + lax.ppermute(send, "item", pair)).astype(BF16)
    partial_rhs = partial_rhs.reshape(n_user, n_chunk, chunk, rank).transpose(1, 0, 2, 3)
    summed = exchange(partial_rhs.reshape(n_chunk, n_user * chunk, rank))
    summed = jnp.sum(summed.astype(F32), axis=0).reshape(n_user, chunk, rank)
    rhs = summed[0]
    for s in range(1, n_user):
        rhs = rhs + over_users(summed[s], s)
    folded = jnp.zeros_like(rhs)
    residual = rhs
    direction = rhs
    spread = jnp.broadcast_to(rhs.astype(BF16)[None], (n_chunk, chunk, rank))

    factors = jnp.concatenate([item_factors, lax.ppermute(item_factors, "item", pair)])
    labels = jnp.concatenate([own_label, far_label])
    pair_own = lax.ppermute(own, "item", pair)
    pair_far = lax.ppermute(far, "item", pair)
    pair_labels = lax.ppermute(labels, "item", pair)
    cells = core * (HG * CBLK) + jnp.arange(HG * CBLK, dtype=jnp.int32)
    code = jnp.arange(1, n_user * cap + 1, dtype=jnp.int32)
    both = jnp.stack([labels, pair_labels])
    table = jnp.sum(jnp.where(both[:, None, :] == cells[None, :, None], code, 0), axis=2) - 1
    table = table.reshape(-1)

    block_flops = 4 * half * blocks * width * rank
    block_bytes = blocks * width * (half + rank) * 2
    plays_shape = (blocks, half, width)
    for number in range(ITERS):
        whole = exchange(spread).reshape(half, rank)
        if number == 0:
            image, plays, reg = call(
                functools.partial(first_kernel, cap, n_items),
                [SMEM, VMEM] + [ANY] * 5,
                [
                    (shape((half, rank), BF16), VMEM),
                    (shape(plays_shape, BF16), VMEM),
                    (shape((half, 128), F32), VMEM),
                ],
                [
                    pltpu.VMEM((blocks * width, rank), BF16),
                    pltpu.VMEM((half, 128), F32),
                    pltpu.VMEM((half, rank), F32),
                    dma((blocks * HG,)),
                    dma((blocks,)),
                ],
                flops=block_flops,
                nbytes=2 * block_bytes,
            )(table, whole, own, far, pair_own, pair_far, factors)
        else:
            last = number == ITERS - 1
            scratch = [
                pltpu.VMEM(plays_shape, BF16),
                pltpu.VMEM((blocks * width, rank), BF16),
                pltpu.VMEM((half, 128 if last else rank), F32),
                dma((blocks,)),
                dma((blocks,)),
            ]
            if last:
                break
            (image,) = call(
                mid_kernel,
                [VMEM, VMEM, ANY, ANY],
                [(shape((half, rank), BF16), VMEM)],
                scratch,
                flops=block_flops,
                nbytes=block_bytes,
            )(whole, reg, plays, factors)
        got = exchange(image.reshape(n_chunk, chunk, rank))
        direction, residual, folded, spread = call(
            vector_kernel,
            [VMEM] * 4,
            [(shape((chunk, rank), F32), VMEM)] * 3 + [(shape((n_chunk, chunk, rank), BF16), VMEM)],
            [],
        )(got, direction, residual, folded)

    (base,) = call(
        base_kernel,
        [VMEM] * 3,
        [(shape((n_item, 16, 128), F32), VMEM)],
        [],
    )(folded, direction, residual)
    (payload,) = call(
        last_kernel,
        [VMEM] * 3 + [ANY] * 2,
        [(shape((n_item, 16, 128), F32), VMEM)],
        scratch,
        flops=block_flops // 2,
        nbytes=block_bytes,
    )(whole, reg, base, plays, factors)
    got = lax.all_to_all(payload, "item", 0, 0, tiled=True)
    (out,) = call(
        final_kernel,
        [VMEM],
        [(shape((HALVES * half, rank // n_item), F32), VMEM)],
        [],
    )(got)
    return out


def solution(mesh):
    placed = (
        P("item", "user", None, None),
        P("item", "user"),
        P("item", "user"),
        P("item", "user"),
        P("item", "user"),
        P("item", None),
    )
    return jax.shard_map(
        shards, mesh=mesh, in_specs=placed, out_specs=P("user", "item"), check_vma=False
    )
```

```python
import functools

import jax
import jax.numpy as jnp
from jax import lax
from jax.experimental import pallas as pl
from jax.experimental.pallas import tpu as pltpu
from jax.sharding import PartitionSpec as P

GROUPS = 8
CBLK = 4
ITERS = 4

EPS = 1.0
GUARD = 1e-06

HALVES = 2
HG = GROUPS // HALVES

BF16 = jnp.bfloat16
F32 = jnp.float32
VMEM = pl.BlockSpec(memory_space=pltpu.VMEM)
SMEM = pl.BlockSpec(memory_space=pltpu.SMEM)
HBM = pl.BlockSpec(memory_space=pltpu.HBM)


def log_tile(counts, rows, cols):
    rank_rows = lax.broadcasted_iota(jnp.int32, counts.shape, 0)
    rank_cols = lax.broadcasted_iota(jnp.int32, counts.shape, 1)
    inside = (rank_rows < rows) & (rank_cols < cols)
    values = jnp.log(1.0 + counts.astype(F32) / EPS)
    return jnp.where(inside, values, 0.0).astype(BF16)


def start_tiles(n_user, cap, own, owner, cell, counts, label, slots, fill, buf, sems):
    total = label.shape[0]
    for s in range(total):
        label[s] = -1
        slots[s] = -1
    for s in range(n_user):
        fill[s] = 0
    me = lax.axis_index("user")

    def visit(t, carry):
        shift = lax.rem(owner[t] - me + n_user, n_user)

        @pl.when((shift == 0) if own else (shift != 0))
        def _():
            base = 0 if own else shift - 1
            k = fill[base]
            slot = base * cap + k
            fill[base] = k + 1
            slots[slot] = t
            label[slot] = cell[t]
            pltpu.make_async_copy(counts.at[t], buf.at[slot], sems.at[slot]).start()

        return carry

    lax.fori_loop(0, counts.shape[0], visit, 0)


def label_rows(label, base, count):
    lane = lax.broadcasted_iota(jnp.int32, (16, 128), 1)
    block = jnp.zeros((16, 128), F32)
    for k in range(count):
        block = jnp.where(lane == k, label[base + k].astype(F32), block)
    return block.astype(BF16)


def pack_kernel(n_user, cap, sizes, owner, cell, rows, cols, counts, *refs):
    parts, (label, slots, fill, buf, logs, cells, sems, out_sems, cell_sems) = refs[: len(sizes)], refs[len(sizes) :]
    start_tiles(n_user, cap, False, owner, cell, counts, label, slots, fill, buf, sems)
    height = counts.shape[1]

    def cells_copy(shift):
        tail = pl.ds(sizes[0] * height, 16)
        return pltpu.make_async_copy(cells.at[shift], parts[0].at[shift, tail, :], cell_sems.at[shift])

    cells[...] = jnp.zeros_like(cells)
    for shift in range(n_user - 1):
        cells[shift, :, 0:128] = label_rows(label, shift * cap, cap)
        cells_copy(shift).start()

    def each(s, act):
        k, shift = lax.rem(s, cap), s // cap
        low = 0
        for part, size in zip(parts, sizes):

            @pl.when((slots[s] >= 0) & (k >= low) & (k < low + size))
            def _(part=part, low=low):
                row = pl.multiple_of((k - low) * height, 16)
                act(pltpu.make_async_copy(logs.at[s], part.at[shift, pl.ds(row, height), :], out_sems.at[s]))

            low += size

    def work(s, carry):
        t = slots[s]

        @pl.when(t >= 0)
        def _():
            pltpu.make_async_copy(counts.at[t], buf.at[s], sems.at[s]).wait()
            logs[s] = log_tile(buf[s], rows[t], cols[t])

        each(s, lambda copy: copy.start())
        return carry

    def finish(s, carry):
        each(s, lambda copy: copy.wait())
        return carry

    lax.fori_loop(0, label.shape[0], work, 0)
    lax.fori_loop(0, label.shape[0], finish, 0)
    for shift in range(n_user - 1):
        cells_copy(shift).wait()


def this_half():
    return lax.rem(lax.axis_index("item"), HALVES)


def rhs_kernel(n_user, cap, sizes, owner, cell, rows, cols, out_label, counts, *refs):
    n = len(sizes)
    parts, (factors, keep, send, tiles, label), bufs = refs[:n], refs[n : n + 5], refs[n + 5 : n + 5 + n]
    slots, fill, buf, logs, dense, sems, out_sems, part_sems = refs[n + 5 + n :]
    start_tiles(n_user, cap, True, owner, cell, counts, label, slots, fill, buf, sems)
    height, width = counts.shape[1], counts.shape[2]
    half = HG * height
    core = this_half()
    moves = [
        pltpu.make_async_copy(part.at[:, pl.ds(0, size * height), :], target, part_sems.at[i])
        for i, (part, target, size) in enumerate(zip(parts, bufs, sizes))
    ]
    for move in moves:
        move.start()
    dense[...] = jnp.zeros_like(dense)

    def put(tile, shift, where):
        group, block = where // CBLK, where % CBLK
        side = jnp.where(group // HG == core, 0, 1)
        row = side * (n_user * half) + shift * half + (group % HG) * height
        one, none = jnp.ones((), BF16), jnp.zeros((), BF16)
        weighted = jnp.where(tile > none, tile + one, none)
        dense[pl.ds(pl.multiple_of(row, 16), height), pl.ds(pl.multiple_of(block * width, 128), width)] = weighted

    low = 0
    for move, source, size in zip(moves, bufs, sizes):
        move.wait()

        def put_sent(s, carry, source=source, size=size, low=low):
            shift, k = s // size, lax.rem(s, size)
            where = out_label[shift * cap + low + k]

            @pl.when(where >= 0)
            def _():
                put(source[shift, pl.ds(pl.multiple_of(k * height, 16), height), :], shift + 1, where)

            return carry

        lax.fori_loop(0, (n_user - 1) * size, put_sent, 0)
        low += size

    def own_copy(s):
        at = pl.ds(pl.multiple_of(s * height, 16), height)
        return pltpu.make_async_copy(logs.at[at], tiles.at[at], out_sems.at[s])

    tail = pl.ds(cap * height, 16)
    tail_copy = pltpu.make_async_copy(logs.at[tail], tiles.at[tail], out_sems.at[cap])
    logs[cap * height :, :] = jnp.zeros((16, width), BF16)
    logs[cap * height :, 0:128] = label_rows(label, 0, cap)
    tail_copy.start()

    def work_own(s, carry):
        t = slots[s]

        @pl.when(t >= 0)
        def _():
            pltpu.make_async_copy(counts.at[t], buf.at[s], sems.at[s]).wait()
            tile = log_tile(buf[s], rows[t], cols[t])
            logs[pl.ds(pl.multiple_of(s * height, 16), height), :] = tile
            own_copy(s).start()
            put(tile, 0, label[s])

        return carry

    def finish_own(s, carry):
        @pl.when(slots[s] >= 0)
        def _():
            own_copy(s).wait()

        return carry

    lax.fori_loop(0, cap, work_own, 0)
    n_chunk = keep.shape[0]
    chunk = half // n_chunk
    for side, target in ((1, send), (0, keep)):

        def dots(s, carry, side=side, target=target):
            row = pl.multiple_of((side * n_user + s) * half, 16)
            part = jnp.dot(dense[pl.ds(row, half), :], factors[...], preferred_element_type=F32)
            at = pl.ds(pl.multiple_of(s * chunk, 8), chunk)
            for k in range(n_chunk):
                target[k, at, :] = part[k * chunk : (k + 1) * chunk, :].astype(target.dtype)
            return carry

        lax.fori_loop(0, n_user, dots, 0)
    lax.fori_loop(0, cap, finish_own, 0)
    tail_copy.wait()


def place_tiles(act, source, label_of, count, plays, first_block, sems, base):
    height = plays.shape[1] // HG
    core = this_half()

    def visit(k, carry):
        where = label_of(k)

        @pl.when((where >= core * (HG * CBLK)) & (where < (core + 1) * (HG * CBLK)))
        def _():
            local = where - core * (HG * CBLK)
            target = plays.at[
                first_block + lax.rem(local, CBLK), pl.ds(pl.multiple_of(local // CBLK * height, 16), height), :
            ]
            tile = source.at[pl.ds(pl.multiple_of(k * height, 16), height), :]
            act(pltpu.make_async_copy(tile, target, sems.at[base + k]))

        return carry

    lax.fori_loop(0, count, visit, 0)


def place_kernel(cap, sizes, own_label, tiles, pair_tiles, *refs):
    n = len(sizes) - 1
    parts, pair_parts = refs[:n], refs[n : 2 * n]
    factors, pair_factors, plays, stacked, labels, raw, whole, raw_sems, label_sem, sems = refs[2 * n :]
    height = plays.shape[1] // HG
    senders = parts[0].shape[0]
    tails = [pair_tiles.at[pl.ds(cap * height, 16), pl.ds(0, 128)]]
    for first in (parts[0], pair_parts[0]):
        for s in range(senders):
            tails.append(first.at[s, pl.ds(sizes[0] * height, 16), pl.ds(0, 128)])
    reads = [pltpu.make_async_copy(tail, raw.at[i], raw_sems.at[i]) for i, tail in enumerate(tails)]
    for read in reads:
        read.start()
    plays[...] = jnp.zeros_like(plays)

    def both(act):
        place_tiles(act, tiles, lambda k: own_label[k], cap, plays, 0, sems, 0)
        place_tiles(act, pair_tiles, lambda k: labels[0, k], cap, plays, CBLK, sems, cap)
        base = 2 * cap
        for side, group in enumerate((parts, pair_parts)):
            for s in range(senders):
                row = 1 + side * senders + s
                low = 0
                for part, size in zip(group, sizes):
                    label_of = lambda k, row=row, low=low: labels[row, low + k]
                    place_tiles(act, part.at[s], label_of, size, plays, side * CBLK, sems, base)
                    low += size
                    base += size

    for i, read in enumerate(reads):
        read.wait()
        whole[i : i + 1, :] = raw[i].astype(F32)[0:1, :].astype(jnp.int32)
    to_scalars = pltpu.make_async_copy(whole, labels, label_sem)
    to_scalars.start()
    items = factors.shape[0]
    stacked[:items, :] = factors[...]
    stacked[items:, :] = pair_factors[...]
    to_scalars.wait()
    both(lambda copy: copy.start())
    both(lambda copy: copy.wait())


def start_kernel(*refs):
    *parts, direction, spread = refs
    rhs = sum(p[...] for p in parts)
    direction[...] = rhs
    low = rhs.astype(BF16)
    for k in range(spread.shape[0]):
        spread[k] = low


def scaled_block(direction, factors, plays):
    projected = lax.dot_general(direction, factors, (((1,), (1,)), ((), ())), preferred_element_type=F32)
    confidence = 1.0 + plays
    return projected, (confidence * projected).astype(BF16)


def lanes(x):
    return sum(x[:, k * 128 : (k + 1) * 128] for k in range(x.shape[1] // 128))


def first_kernel(
    n_items, offset, labels, direction, placed, late, pair_late, factors, image, plays, reg, seen, acc, buf, sems
):
    senders, height = late.shape[0], plays.shape[1] // HG
    size = late.shape[1] // height
    moves = [pltpu.make_async_copy(part, buf.at[i], sems.at[i]) for i, part in enumerate((late, pair_late))]
    for move in moves:
        move.start()
    plays[...] = placed[...]
    core = this_half()
    for side, move in enumerate(moves):
        move.wait()

        def visit(i, carry, side=side):
            s, k = i // size, lax.rem(i, size)
            where = labels[1 + side * senders + s, offset + k]

            @pl.when((where >= core * (HG * CBLK)) & (where < (core + 1) * (HG * CBLK)))
            def _():
                local = where - core * (HG * CBLK)
                row = pl.ds(pl.multiple_of(local // CBLK * height, 16), height)
                tile = buf[side, s, pl.ds(pl.multiple_of(k * height, 16), height), :]
                plays[side * CBLK + lax.rem(local, CBLK), row, :] = tile

            return carry

        lax.fori_loop(0, senders * size, visit, 0)
    blocks, _, width = plays.shape
    for j in range(blocks):
        block = factors[j * width : (j + 1) * width, :]
        value = plays[j].astype(F32)
        _, scaled = scaled_block(direction[...], block, value)
        part = jnp.dot(scaled, block, preferred_element_type=F32)
        count = lanes(jnp.where(value > 0, 1.0, 0.0))
        if j == 0:
            acc[...] = part
            seen[...] = count
        else:
            acc[...] += part
            seen[...] += count
    share = jnp.sum(seen[...], axis=1, keepdims=True) / n_items
    reg[...] = jnp.broadcast_to(share, reg.shape)
    image[...] = (acc[...] + share * direction[...].astype(F32)).astype(BF16)


def mid_kernel(direction, reg, plays, factors, image, acc):
    blocks, _, width = plays.shape
    for j in range(blocks):
        block = factors[j * width : (j + 1) * width, :]
        _, scaled = scaled_block(direction[...], block, plays[j].astype(F32))
        part = jnp.dot(scaled, block, preferred_element_type=F32)
        if j == 0:
            acc[...] = part
        else:
            acc[...] += part
    image[...] = (acc[...] + reg[:, :1] * direction[...].astype(F32)).astype(BF16)


def last_kernel(direction, reg, base, plays, factors, payload, acc, laid):
    blocks, _, width = plays.shape
    for j in range(blocks):
        block = factors[j * width : (j + 1) * width, :]
        projected, scaled = scaled_block(direction[...], block, plays[j].astype(F32))
        part = lanes(scaled.astype(F32) * projected)
        if j == 0:
            acc[...] = part
        else:
            acc[...] += part
    wide = direction[...].astype(F32)
    along = acc[...] + reg[:, :1] * lanes(wide * wide)
    along = jnp.broadcast_to(jnp.sum(along, axis=1, keepdims=True), acc.shape)
    laid[...] = jnp.zeros_like(laid)
    n_item = base.shape[0]
    first, free = free_lanes(acc.shape[0] * HALVES // n_item)
    put_row(laid, 0, as_row(along), first, free)
    for i in range(n_item):
        payload[i] = base[i] + laid[...]


def free_lanes(chunk):
    return 2 * chunk, 128 - 2 * chunk


def as_row(column):
    n = column.shape[0]
    return jnp.concatenate([column[k : min(k + 128, n), :].T[0:1, :] for k in range(0, n, 128)], axis=1)


def put_row(target, row, values, first, free):
    n = values.shape[1]
    for k in range(0, n, free):
        m = min(free, n - k)
        target[row + k // free : row + k // free + 1, first : first + m] = values[:, k : k + m]


def get_row(source, row, n, first, free):
    pieces = [source[row + k // free : row + k // free + 1, first : first + min(free, n - k)] for k in range(0, n, free)]
    return jnp.concatenate(pieces, axis=1)


def lay_base(folded, direction, residual, base):
    n_item, share, _ = base.shape
    chunk = folded.shape[0]
    first, free = free_lanes(chunk)
    base[...] = jnp.zeros_like(base)
    norm = jnp.sum(residual * residual, axis=1, keepdims=True)
    norm = as_row(jnp.broadcast_to(norm, (chunk, 128)))
    sides = (folded.T, direction.T)
    row = n_item // HALVES * chunk // free
    for i in range(n_item):
        for k in range(2):
            base[i, :, k * chunk : (k + 1) * chunk] = sides[k][i * share : (i + 1) * share, :]
        put_row(base.at[i], row, norm, first, free)


def final_kernel(got, out):
    n_item = got.shape[0]
    n_chunk = n_item // HALVES
    half = out.shape[1] // HALVES
    chunk = half // n_chunk
    first, free = free_lanes(chunk)
    for h in range(HALVES):
        sources = [got[k * HALVES + h] for k in range(n_chunk)]
        along = get_row(sum(sources), 0, half, first, free)
        norm = jnp.concatenate([get_row(x, half // free, chunk, first, free) for x in sources], axis=1)
        alpha = norm / (along + GUARD)
        for k, x in enumerate(sources):
            at = slice(k * chunk, (k + 1) * chunk)
            out[:, h * half + k * chunk : h * half + (k + 1) * chunk] = x[:, :chunk] + alpha[:, at] * x[:, chunk : 2 * chunk]


def vector_kernel(number, got, direction, residual, folded, spread, *outs):
    image = sum(got[k].astype(F32) for k in range(got.shape[0]))
    d, r = direction[...], residual[...]
    norm = jnp.sum(r * r, axis=1, keepdims=True)
    alpha = norm / (jnp.sum(d * image, axis=1, keepdims=True) + GUARD)
    step = alpha * d
    total = folded[...] + step if number else step
    r = r - alpha * image
    fresh = jnp.sum(r * r, axis=1, keepdims=True)
    d = r + fresh / (norm + GUARD) * d
    low = d.astype(BF16)
    for k in range(spread.shape[0]):
        spread[k] = low
    if len(outs) == 1:
        lay_base(total, d, r, outs[0])
    else:
        outs[0][...], outs[1][...], outs[2][...] = d, r, total


def shards(play_counts, tile_owner, tile_cell, tile_rows, tile_cols, item_factors):
    counts = play_counts[0]
    tiles_dev, height, width = counts.shape
    n_user = lax.axis_size("user")
    n_item = lax.axis_size("item")
    shard_items, rank = item_factors.shape
    cap = GROUPS * CBLK // n_user
    n_out = (n_user - 1) * cap
    n_chunk = n_item // HALVES
    half = HG * height
    chunk = half // n_chunk
    n_items = float(shard_items * n_item)
    blocks = HALVES * CBLK
    pair = [(i, i ^ 1) for i in range(n_item)]
    groups = [[h + HALVES * k for k in range(n_chunk)] for h in range(HALVES)]

    def shape(dims, dtype):
        return jax.ShapeDtypeStruct(dims, dtype)

    def call(kernel, ins, outs, scratch, grant, flops=0, nbytes=0, aliases=None):
        return pl.pallas_call(
            kernel,
            out_shape=[o[0] for o in outs],
            in_specs=ins,
            out_specs=[o[1] for o in outs],
            scratch_shapes=scratch,
            input_output_aliases=aliases or {},
            compiler_params=pltpu.CompilerParams(vmem_limit_bytes=grant * 2**20),
            cost_estimate=pl.CostEstimate(flops=flops, bytes_accessed=nbytes, transcendentals=0),
        )

    def over_users(x, shift):
        return lax.ppermute(x, "user", [(u, (u + shift) % n_user) for u in range(n_user)])

    def from_users(x):
        got = [over_users(x[s - 1 : s], s) for s in range(1, n_user)]
        return jnp.concatenate(got) if n_user > 2 else got[0]

    def to_pair(x):
        return lax.ppermute(x, "item", pair)

    def exchange(x):
        return lax.all_to_all(x, "item", 0, 0, axis_index_groups=groups, tiled=True)

    route = (tile_owner[0], tile_cell[0], tile_rows[0], tile_cols[0])
    dma = pltpu.SemaphoreType.DMA
    sizes = [cap - cap // 4, cap // 4]
    part_shapes = [(n_user - 1, size * height, width) for size in sizes]
    sent_shapes = [(n_user - 1, size * height + (0 if i else 16), width) for i, size in enumerate(sizes)]
    *parts, out_label = call(
        functools.partial(pack_kernel, n_user, cap, sizes),
        [SMEM] * 4 + [HBM],
        [(shape(sent, BF16), HBM) for sent in sent_shapes] + [(shape((n_out,), jnp.int32), SMEM)],
        [
            pltpu.SMEM((n_out,), jnp.int32),
            pltpu.SMEM((n_user,), jnp.int32),
            pltpu.VMEM((n_out, height, width), jnp.int32),
            pltpu.VMEM((n_out, height, width), BF16),
            pltpu.VMEM((n_user - 1, 16, width), BF16),
            dma((n_out,)),
            dma((n_out,)),
            dma((n_user - 1,)),
        ],
        56,
        nbytes=n_out * height * width * 6,
    )(*route, counts)
    far = [from_users(part) for part in parts[:-1]]
    pair_factors = to_pair(item_factors)

    state = (n_chunk, n_user * chunk, rank)
    keep, send, own, own_label = call(
        functools.partial(rhs_kernel, n_user, cap, sizes),
        [SMEM] * 5 + [HBM] * (1 + len(sizes)) + [VMEM],
        [
            (pltpu.VMEM(state, F32), VMEM),
            (pltpu.VMEM(state, BF16), VMEM),
            (shape((cap * height + 16, width), BF16), HBM),
            (shape((cap,), jnp.int32), SMEM),
        ],
        [pltpu.VMEM(part, BF16) for part in part_shapes]
        + [
            pltpu.SMEM((cap,), jnp.int32),
            pltpu.SMEM((n_user,), jnp.int32),
            pltpu.VMEM((cap, height, width), jnp.int32),
            pltpu.VMEM((cap * height + 16, width), BF16),
            pltpu.VMEM((HALVES * n_user * half, shard_items), BF16),
            dma((cap,)),
            dma((cap + 1,)),
            dma((len(sizes),)),
        ],
        56,
        flops=2 * HALVES * n_user * half * shard_items * rank,
        nbytes=2 * tiles_dev * height * width * 4,
    )(*route, out_label, counts, *parts, item_factors)

    summed = exchange((keep + to_pair(send).astype(F32)).astype(BF16))
    pair_own = to_pair(own)
    summed = jnp.sum(summed.astype(F32), axis=0).reshape(n_user, chunk, rank)
    terms = [summed[0]] + [over_users(summed[s], s) for s in range(1, n_user)]
    direction, spread = call(
        start_kernel,
        [VMEM] * n_user,
        [(shape((chunk, rank), F32), VMEM), (shape((n_chunk, chunk, rank), BF16), VMEM)],
        [],
        4,
    )(*terms)
    residual = folded = direction
    last_part, spread = lax.optimization_barrier((parts[-1], spread))
    late = from_users(last_part)
    pair_parts = [to_pair(part) for part in far]
    plays_shape = (blocks, half, width)
    n_labels = 2 * (n_user - 1) + 1
    label_shape = (-(-n_labels // 8) * 8, 128)
    placed, factors, labels = call(
        functools.partial(place_kernel, cap, sizes),
        [SMEM] + [HBM] * (2 + 2 * len(far)) + [VMEM] * 2,
        [
            (pltpu.VMEM(plays_shape, BF16), VMEM),
            (pltpu.VMEM((HALVES * shard_items, rank), BF16), VMEM),
            (shape(label_shape, jnp.int32), SMEM),
        ],
        [
            pltpu.VMEM((n_labels, 16, 128), BF16),
            pltpu.VMEM(label_shape, jnp.int32),
            dma((n_labels,)),
            dma(()),
            dma((2 * n_user * cap,)),
        ],
        50,
        nbytes=2 * blocks * half * width,
    )(own_label, own, pair_own, *far, *pair_parts, item_factors, pair_factors)

    block_flops = 4 * half * blocks * width * rank
    block_bytes = blocks * width * (half + rank) * 2
    share = rank // n_item
    payload_shape = shape((n_item, share, 128), F32)
    image_out = (shape((half, rank), BF16), VMEM)
    for number in range(ITERS):
        whole = exchange(spread).reshape(half, rank)
        if number == ITERS - 1:
            break
        if number == 0:
            late, whole, labels = lax.optimization_barrier((late, whole, labels))
            pair_late = to_pair(late)
            image, plays, reg = call(
                functools.partial(first_kernel, n_items, cap - sizes[-1]),
                [SMEM] + [VMEM] * 2 + [HBM] * 2 + [VMEM],
                [image_out, (pltpu.VMEM(plays_shape, BF16), VMEM), (shape((half, 128), F32), VMEM)],
                [
                    pltpu.VMEM((half, 128), F32),
                    pltpu.VMEM((half, rank), F32),
                    pltpu.VMEM((2, *part_shapes[-1]), BF16),
                    dma((2,)),
                ],
                20,
                flops=block_flops,
                nbytes=2 * block_bytes,
            )(labels, whole, placed, late, pair_late, factors)
        else:
            (image,) = call(
                mid_kernel,
                [VMEM] * 4,
                [image_out],
                [pltpu.VMEM((half, rank), F32)],
                12,
                flops=block_flops,
                nbytes=block_bytes,
            )(whole, reg, plays, factors)
        got = exchange(image.reshape(n_chunk, chunk, rank))
        ends = number == ITERS - 2
        outs = [(payload_shape, VMEM)] if ends else [(shape((chunk, rank), F32), VMEM)] * 3
        spread, *outs = call(
            functools.partial(vector_kernel, number),
            [VMEM] * 4,
            [(shape((n_chunk, chunk, rank), BF16), VMEM)] + outs,
            [],
            4,
        )(got, direction, residual, folded)
        if ends:
            (base,) = outs
        else:
            direction, residual, folded = outs

    (payload,) = call(
        last_kernel,
        [VMEM] * 5,
        [(payload_shape, VMEM)],
        [pltpu.VMEM((half, 128), F32), pltpu.VMEM((share, 128), F32)],
        12,
        flops=block_flops // 2,
        nbytes=block_bytes,
    )(whole, reg, base, plays, factors)
    got = lax.all_to_all(payload, "item", 0, 0, tiled=True)
    (out,) = call(final_kernel, [VMEM], [(shape((share, HALVES * half), F32), VMEM)], [], 4)(got)
    return out.T


def solution(mesh):
    placed = (
        P("item", "user", None, None),
        P("item", "user"),
        P("item", "user"),
        P("item", "user"),
        P("item", "user"),
        P("item", None),
    )
    return jax.shard_map(
        shards, mesh=mesh, in_specs=placed, out_specs=P("user", "item"), check_vma=False
    )
```

```python
import functools

import jax
import jax.numpy as jnp
from jax import lax
from jax.experimental import pallas as pl
from jax.experimental.pallas import tpu as pltpu
from jax.sharding import PartitionSpec as P

GROUPS = 8
CBLK = 4
ITERS = 4

EPS = 1.0
GUARD = 1e-06

HALVES = 2
HG = GROUPS // HALVES

BF16 = jnp.bfloat16
F32 = jnp.float32
VMEM = pl.BlockSpec(memory_space=pltpu.VMEM)
SMEM = pl.BlockSpec(memory_space=pltpu.SMEM)
HBM = pl.BlockSpec(memory_space=pltpu.HBM)


def log_tile(counts, rows, cols):
    height, width = counts.shape
    in_rows = (lax.broadcasted_iota(jnp.int32, (height, 1), 0) < rows).astype(F32)
    in_cols = (lax.broadcasted_iota(jnp.int32, (1, width), 1) < cols).astype(F32)
    return jnp.log(1.0 + counts.astype(F32) / EPS * in_cols * in_rows).astype(BF16)


def start_tiles(n_user, cap, own, owner, cell, counts, label, slots, fill, buf, sems):
    total = label.shape[0]
    for s in range(total):
        label[s] = -1
        slots[s] = -1
    for s in range(n_user):
        fill[s] = 0
    me = lax.axis_index("user")

    def visit(t, carry):
        shift = lax.rem(owner[t] - me + n_user, n_user)

        @pl.when((shift == 0) if own else (shift != 0))
        def _():
            base = 0 if own else shift - 1
            k = fill[base]
            slot = base * cap + k
            fill[base] = k + 1
            slots[slot] = t
            label[slot] = cell[t]
            pltpu.make_async_copy(counts.at[t], buf.at[slot], sems.at[slot]).start()

        return carry

    lax.fori_loop(0, counts.shape[0], visit, 0)


def label_rows(label, base, count):
    lane = lax.broadcasted_iota(jnp.int32, (16, 128), 1)
    block = jnp.zeros((16, 128), F32)
    for k in range(count):
        block = jnp.where(lane == k, label[base + k].astype(F32), block)
    return block.astype(BF16)


def pack_kernel(n_user, cap, sizes, owner, cell, rows, cols, counts, *refs):
    parts, (label, slots, fill, buf, logs, cells, sems, out_sems, cell_sems) = refs[: len(sizes)], refs[len(sizes) :]
    start_tiles(n_user, cap, False, owner, cell, counts, label, slots, fill, buf, sems)
    height = counts.shape[1]

    def cells_copy(shift):
        tail = pl.ds(sizes[0] * height, 16)
        return pltpu.make_async_copy(cells.at[shift], parts[0].at[shift, tail, :], cell_sems.at[shift])

    cells[...] = jnp.zeros_like(cells)
    for shift in range(n_user - 1):
        cells[shift, :, 0:128] = label_rows(label, shift * cap, cap)
        cells_copy(shift).start()

    def each(s, act):
        k, shift = lax.rem(s, cap), s // cap
        low = 0
        for part, size in zip(parts, sizes):

            @pl.when((slots[s] >= 0) & (k >= low) & (k < low + size))
            def _(part=part, low=low):
                row = pl.multiple_of((k - low) * height, 16)
                act(pltpu.make_async_copy(logs.at[s], part.at[shift, pl.ds(row, height), :], out_sems.at[s]))

            low += size

    def work(s, carry):
        t = slots[s]

        @pl.when(t >= 0)
        def _():
            pltpu.make_async_copy(counts.at[t], buf.at[s], sems.at[s]).wait()
            logs[s] = log_tile(buf[s], rows[t], cols[t])

        each(s, lambda copy: copy.start())
        return carry

    def finish(s, carry):
        each(s, lambda copy: copy.wait())
        return carry

    lax.fori_loop(0, label.shape[0], work, 0)
    lax.fori_loop(0, label.shape[0], finish, 0)
    for shift in range(n_user - 1):
        cells_copy(shift).wait()


def this_half():
    return lax.rem(lax.axis_index("item"), HALVES)


def rhs_kernel(n_user, cap, sizes, owner, cell, rows, cols, out_label, counts, *refs):
    n = len(sizes)
    parts, (factors, keep, send, tiles, label), bufs = refs[:n], refs[n : n + 5], refs[n + 5 : n + 5 + n]
    slots, fill, buf, logs, dense, sems, out_sems, part_sems = refs[n + 5 + n :]
    start_tiles(n_user, cap, True, owner, cell, counts, label, slots, fill, buf, sems)
    height, width = counts.shape[1], counts.shape[2]
    half = HG * height
    core = this_half()
    moves = [
        pltpu.make_async_copy(part.at[:, pl.ds(0, size * height), :], target, part_sems.at[i])
        for i, (part, target, size) in enumerate(zip(parts, bufs, sizes))
    ]
    for move in moves:
        move.start()
    dense[...] = jnp.zeros_like(dense)

    def put(tile, shift, where):
        group, block = where // CBLK, where % CBLK
        side = jnp.where(group // HG == core, 0, 1)
        row = side * (n_user * half) + shift * half + (group % HG) * height
        one, none = jnp.ones((), BF16), jnp.zeros((), BF16)
        weighted = jnp.where(tile > none, tile + one, none)
        dense[pl.ds(pl.multiple_of(row, 16), height), pl.ds(pl.multiple_of(block * width, 128), width)] = weighted

    low = 0
    for move, source, size in zip(moves, bufs, sizes):
        move.wait()

        def put_sent(s, carry, source=source, size=size, low=low):
            shift, k = s // size, lax.rem(s, size)
            where = out_label[shift * cap + low + k]

            @pl.when(where >= 0)
            def _():
                put(source[shift, pl.ds(pl.multiple_of(k * height, 16), height), :], shift + 1, where)

            return carry

        lax.fori_loop(0, (n_user - 1) * size, put_sent, 0)
        low += size

    def own_copy(s):
        at = pl.ds(pl.multiple_of(s * height, 16), height)
        return pltpu.make_async_copy(logs.at[at], tiles.at[at], out_sems.at[s])

    tail = pl.ds(cap * height, 16)
    tail_copy = pltpu.make_async_copy(logs.at[tail], tiles.at[tail], out_sems.at[cap])
    logs[cap * height :, :] = jnp.zeros((16, width), BF16)
    logs[cap * height :, 0:128] = label_rows(label, 0, cap)
    tail_copy.start()

    def work_own(s, carry):
        t = slots[s]

        @pl.when(t >= 0)
        def _():
            pltpu.make_async_copy(counts.at[t], buf.at[s], sems.at[s]).wait()
            tile = log_tile(buf[s], rows[t], cols[t])
            logs[pl.ds(pl.multiple_of(s * height, 16), height), :] = tile
            own_copy(s).start()
            put(tile, 0, label[s])

        return carry

    def finish_own(s, carry):
        @pl.when(slots[s] >= 0)
        def _():
            own_copy(s).wait()

        return carry

    lax.fori_loop(0, cap, work_own, 0)
    n_chunk = keep.shape[0]
    chunk = half // n_chunk
    for side, target in ((1, send), (0, keep)):

        def dots(s, carry, side=side, target=target):
            row = pl.multiple_of((side * n_user + s) * half, 16)
            part = jnp.dot(dense[pl.ds(row, half), :], factors[...], preferred_element_type=F32)
            at = pl.ds(pl.multiple_of(s * chunk, 8), chunk)
            for k in range(n_chunk):
                target[k, at, :] = part[k * chunk : (k + 1) * chunk, :].astype(target.dtype)
            return carry

        lax.fori_loop(0, n_user, dots, 0)
    lax.fori_loop(0, cap, finish_own, 0)
    tail_copy.wait()


def place_tiles(act, source, label_of, count, plays, first_block, sems, base):
    height = plays.shape[1] // HG
    core = this_half()

    def visit(k, carry):
        where = label_of(k)

        @pl.when((where >= core * (HG * CBLK)) & (where < (core + 1) * (HG * CBLK)))
        def _():
            local = where - core * (HG * CBLK)
            target = plays.at[
                first_block + lax.rem(local, CBLK), pl.ds(pl.multiple_of(local // CBLK * height, 16), height), :
            ]
            tile = source.at[pl.ds(pl.multiple_of(k * height, 16), height), :]
            act(pltpu.make_async_copy(tile, target, sems.at[base + k]))

        return carry

    lax.fori_loop(0, count, visit, 0)


def place_kernel(cap, sizes, own_label, tiles, pair_tiles, *refs):
    n = len(sizes) - 1
    parts, pair_parts = refs[:n], refs[n : 2 * n]
    factors, pair_factors, plays, stacked, labels, raw, whole, raw_sems, label_sem, sems = refs[2 * n :]
    height = plays.shape[1] // HG
    senders = parts[0].shape[0]
    tails = [pair_tiles.at[pl.ds(cap * height, 16), pl.ds(0, 128)]]
    for first in (parts[0], pair_parts[0]):
        for s in range(senders):
            tails.append(first.at[s, pl.ds(sizes[0] * height, 16), pl.ds(0, 128)])
    reads = [pltpu.make_async_copy(tail, raw.at[i], raw_sems.at[i]) for i, tail in enumerate(tails)]
    for read in reads:
        read.start()
    plays[...] = jnp.zeros_like(plays)

    def own(act):
        place_tiles(act, tiles, lambda k: own_label[k], cap, plays, 0, sems, 0)

    def others(act):
        place_tiles(act, pair_tiles, lambda k: labels[0, k], cap, plays, CBLK, sems, cap)
        base = 2 * cap
        for side, group in enumerate((parts, pair_parts)):
            for s in range(senders):
                row = 1 + side * senders + s
                low = 0
                for part, size in zip(group, sizes):
                    label_of = lambda k, row=row, low=low: labels[row, low + k]
                    place_tiles(act, part.at[s], label_of, size, plays, side * CBLK, sems, base)
                    low += size
                    base += size

    own(lambda copy: copy.start())
    for i, read in enumerate(reads):
        read.wait()
        whole[i : i + 1, :] = raw[i].astype(F32)[0:1, :].astype(jnp.int32)
    to_scalars = pltpu.make_async_copy(whole, labels, label_sem)
    to_scalars.start()
    items = factors.shape[0]
    stacked[:items, :] = factors[...]
    stacked[items:, :] = pair_factors[...]
    to_scalars.wait()
    others(lambda copy: copy.start())
    own(lambda copy: copy.wait())
    others(lambda copy: copy.wait())


def start_kernel(*refs):
    *parts, direction, spread = refs
    rhs = sum(p[...] for p in parts)
    direction[...] = rhs
    low = rhs.astype(BF16)
    for k in range(spread.shape[0]):
        spread[k] = low


def scaled_block(direction, factors, plays):
    projected = lax.dot_general(direction, factors, (((1,), (1,)), ((), ())), preferred_element_type=F32)
    confidence = 1.0 + plays
    return projected, (confidence * projected).astype(BF16)


def lanes(x):
    return sum(x[:, k * 128 : (k + 1) * 128] for k in range(x.shape[1] // 128))


def first_kernel(
    n_items, offset, labels, direction, placed, late, pair_late, factors, image, plays, reg, seen, acc, buf, sems
):
    senders, height = late.shape[0], plays.shape[1] // HG
    size = late.shape[1] // height
    moves = [pltpu.make_async_copy(part, buf.at[i], sems.at[i]) for i, part in enumerate((late, pair_late))]
    for move in moves:
        move.start()
    plays[...] = placed[...]
    core = this_half()
    for side, move in enumerate(moves):
        move.wait()

        def visit(i, carry, side=side):
            s, k = i // size, lax.rem(i, size)
            where = labels[1 + side * senders + s, offset + k]

            @pl.when((where >= core * (HG * CBLK)) & (where < (core + 1) * (HG * CBLK)))
            def _():
                local = where - core * (HG * CBLK)
                row = pl.ds(pl.multiple_of(local // CBLK * height, 16), height)
                tile = buf[side, s, pl.ds(pl.multiple_of(k * height, 16), height), :]
                plays[side * CBLK + lax.rem(local, CBLK), row, :] = tile

            return carry

        lax.fori_loop(0, senders * size, visit, 0)
    blocks, _, width = plays.shape
    for j in range(blocks):
        block = factors[j * width : (j + 1) * width, :]
        value = plays[j].astype(F32)
        _, scaled = scaled_block(direction[...], block, value)
        part = jnp.dot(scaled, block, preferred_element_type=F32)
        count = lanes(jnp.where(value > 0, 1.0, 0.0))
        if j == 0:
            acc[...] = part
            seen[...] = count
        else:
            acc[...] += part
            seen[...] += count
    share = jnp.sum(seen[...], axis=1, keepdims=True) / n_items
    reg[...] = jnp.broadcast_to(share, reg.shape)
    image[...] = (acc[...] + share * direction[...].astype(F32)).astype(BF16)


def mid_kernel(direction, reg, plays, factors, image, acc):
    blocks, _, width = plays.shape
    for j in range(blocks):
        block = factors[j * width : (j + 1) * width, :]
        _, scaled = scaled_block(direction[...], block, plays[j].astype(F32))
        part = jnp.dot(scaled, block, preferred_element_type=F32)
        if j == 0:
            acc[...] = part
        else:
            acc[...] += part
    image[...] = (acc[...] + reg[:, :1] * direction[...].astype(F32)).astype(BF16)


def last_kernel(direction, reg, base, plays, factors, payload, acc, laid):
    blocks, _, width = plays.shape
    for j in range(blocks):
        block = factors[j * width : (j + 1) * width, :]
        projected, scaled = scaled_block(direction[...], block, plays[j].astype(F32))
        part = lanes(scaled.astype(F32) * projected)
        if j == 0:
            acc[...] = part
        else:
            acc[...] += part
    wide = direction[...].astype(F32)
    along = acc[...] + reg[:, :1] * lanes(wide * wide)
    along = jnp.broadcast_to(jnp.sum(along, axis=1, keepdims=True), acc.shape)
    laid[...] = jnp.zeros_like(laid)
    n_item = base.shape[0]
    first, free = free_lanes(acc.shape[0] * HALVES // n_item)
    put_row(laid, 0, as_row(along), first, free)
    for i in range(n_item):
        payload[i] = base[i] + laid[...]


def free_lanes(chunk):
    return 2 * chunk, 128 - 2 * chunk


def as_row(column):
    n = column.shape[0]
    return jnp.concatenate([column[k : min(k + 128, n), :].T[0:1, :] for k in range(0, n, 128)], axis=1)


def put_row(target, row, values, first, free):
    n = values.shape[1]
    for k in range(0, n, free):
        m = min(free, n - k)
        target[row + k // free : row + k // free + 1, first : first + m] = values[:, k : k + m]


def get_row(source, row, n, first, free):
    pieces = [source[row + k // free : row + k // free + 1, first : first + min(free, n - k)] for k in range(0, n, free)]
    return jnp.concatenate(pieces, axis=1)


def lay_base(folded, direction, residual, base):
    n_item, share, _ = base.shape
    chunk = folded.shape[0]
    first, free = free_lanes(chunk)
    base[...] = jnp.zeros_like(base)
    norm = jnp.sum(residual * residual, axis=1, keepdims=True)
    norm = as_row(jnp.broadcast_to(norm, (chunk, 128)))
    sides = (folded.T, direction.T)
    row = n_item // HALVES * chunk // free
    for i in range(n_item):
        for k in range(2):
            base[i, :, k * chunk : (k + 1) * chunk] = sides[k][i * share : (i + 1) * share, :]
        put_row(base.at[i], row, norm, first, free)


def final_kernel(got, out):
    n_item = got.shape[0]
    n_chunk = n_item // HALVES
    half = out.shape[1] // HALVES
    chunk = half // n_chunk
    first, free = free_lanes(chunk)
    for h in range(HALVES):
        sources = [got[k * HALVES + h] for k in range(n_chunk)]
        along = get_row(sum(sources), 0, half, first, free)
        norm = jnp.concatenate([get_row(x, half // free, chunk, first, free) for x in sources], axis=1)
        alpha = norm / (along + GUARD)
        for k, x in enumerate(sources):
            at = slice(k * chunk, (k + 1) * chunk)
            out[:, h * half + k * chunk : h * half + (k + 1) * chunk] = x[:, :chunk] + alpha[:, at] * x[:, chunk : 2 * chunk]


def vector_kernel(number, got, direction, residual, folded, spread, *outs):
    image = sum(got[k].astype(F32) for k in range(got.shape[0]))
    d, r = direction[...], residual[...]
    norm = jnp.sum(r * r, axis=1, keepdims=True)
    alpha = norm / (jnp.sum(d * image, axis=1, keepdims=True) + GUARD)
    step = alpha * d
    total = folded[...] + step if number else step
    r = r - alpha * image
    fresh = jnp.sum(r * r, axis=1, keepdims=True)
    d = r + fresh / (norm + GUARD) * d
    low = d.astype(BF16)
    for k in range(spread.shape[0]):
        spread[k] = low
    if len(outs) == 1:
        lay_base(total, d, r, outs[0])
    else:
        outs[0][...], outs[1][...], outs[2][...] = d, r, total


def shards(play_counts, tile_owner, tile_cell, tile_rows, tile_cols, item_factors):
    counts = play_counts[0]
    tiles_dev, height, width = counts.shape
    n_user = lax.axis_size("user")
    n_item = lax.axis_size("item")
    shard_items, rank = item_factors.shape
    cap = GROUPS * CBLK // n_user
    n_out = (n_user - 1) * cap
    n_chunk = n_item // HALVES
    half = HG * height
    chunk = half // n_chunk
    n_items = float(shard_items * n_item)
    blocks = HALVES * CBLK
    pair = [(i, i ^ 1) for i in range(n_item)]
    groups = [[h + HALVES * k for k in range(n_chunk)] for h in range(HALVES)]

    def shape(dims, dtype):
        return jax.ShapeDtypeStruct(dims, dtype)

    def call(kernel, ins, outs, scratch, grant, flops=0, nbytes=0, aliases=None):
        return pl.pallas_call(
            kernel,
            out_shape=[o[0] for o in outs],
            in_specs=ins,
            out_specs=[o[1] for o in outs],
            scratch_shapes=scratch,
            input_output_aliases=aliases or {},
            compiler_params=pltpu.CompilerParams(vmem_limit_bytes=grant * 2**20),
            cost_estimate=pl.CostEstimate(flops=flops, bytes_accessed=nbytes, transcendentals=0),
        )

    def over_users(x, shift):
        return lax.ppermute(x, "user", [(u, (u + shift) % n_user) for u in range(n_user)])

    def from_users(x):
        got = [over_users(x[s - 1 : s], s) for s in range(1, n_user)]
        return jnp.concatenate(got) if n_user > 2 else got[0]

    def to_pair(x):
        return lax.ppermute(x, "item", pair)

    def exchange(x):
        return lax.all_to_all(x, "item", 0, 0, axis_index_groups=groups, tiled=True)

    route = (tile_owner[0], tile_cell[0], tile_rows[0], tile_cols[0])
    dma = pltpu.SemaphoreType.DMA
    sizes = [cap - cap // 4, cap // 4]
    part_shapes = [(n_user - 1, size * height, width) for size in sizes]
    sent_shapes = [(n_user - 1, size * height + (0 if i else 16), width) for i, size in enumerate(sizes)]
    *parts, out_label = call(
        functools.partial(pack_kernel, n_user, cap, sizes),
        [SMEM] * 4 + [HBM],
        [(shape(sent, BF16), HBM) for sent in sent_shapes] + [(shape((n_out,), jnp.int32), SMEM)],
        [
            pltpu.SMEM((n_out,), jnp.int32),
            pltpu.SMEM((n_user,), jnp.int32),
            pltpu.VMEM((n_out, height, width), jnp.int32),
            pltpu.VMEM((n_out, height, width), BF16),
            pltpu.VMEM((n_user - 1, 16, width), BF16),
            dma((n_out,)),
            dma((n_out,)),
            dma((n_user - 1,)),
        ],
        56,
        nbytes=n_out * height * width * 6,
    )(*route, counts)
    far = [from_users(part) for part in parts[:-1]]
    pair_factors = to_pair(item_factors)

    state = (n_chunk, n_user * chunk, rank)
    keep, send, own, own_label = call(
        functools.partial(rhs_kernel, n_user, cap, sizes),
        [SMEM] * 5 + [HBM] * (1 + len(sizes)) + [VMEM],
        [
            (pltpu.VMEM(state, F32), VMEM),
            (pltpu.VMEM(state, BF16), VMEM),
            (shape((cap * height + 16, width), BF16), HBM),
            (shape((cap,), jnp.int32), SMEM),
        ],
        [pltpu.VMEM(part, BF16) for part in part_shapes]
        + [
            pltpu.SMEM((cap,), jnp.int32),
            pltpu.SMEM((n_user,), jnp.int32),
            pltpu.VMEM((cap, height, width), jnp.int32),
            pltpu.VMEM((cap * height + 16, width), BF16),
            pltpu.VMEM((HALVES * n_user * half, shard_items), BF16),
            dma((cap,)),
            dma((cap + 1,)),
            dma((len(sizes),)),
        ],
        56,
        flops=2 * HALVES * n_user * half * shard_items * rank,
        nbytes=2 * tiles_dev * height * width * 4,
    )(*route, out_label, counts, *parts, item_factors)

    summed = exchange((keep + to_pair(send).astype(F32)).astype(BF16))
    pair_own = to_pair(own)
    summed = jnp.sum(summed.astype(F32), axis=0).reshape(n_user, chunk, rank)
    last_part, summed = lax.optimization_barrier((parts[-1], summed))
    terms = [summed[0]] + [over_users(summed[s], s) for s in range(1, n_user)]
    direction, spread = call(
        start_kernel,
        [VMEM] * n_user,
        [(shape((chunk, rank), F32), VMEM), (shape((n_chunk, chunk, rank), BF16), VMEM)],
        [],
        4,
    )(*terms)
    residual = folded = direction
    late = from_users(last_part)
    pair_parts = [to_pair(part) for part in far]
    plays_shape = (blocks, half, width)
    n_labels = 2 * (n_user - 1) + 1
    label_shape = (-(-n_labels // 8) * 8, 128)
    placed, factors, labels = call(
        functools.partial(place_kernel, cap, sizes),
        [SMEM] + [HBM] * (2 + 2 * len(far)) + [VMEM] * 2,
        [
            (shape(plays_shape, BF16), VMEM),
            (pltpu.VMEM((HALVES * shard_items, rank), BF16), VMEM),
            (shape(label_shape, jnp.int32), SMEM),
        ],
        [
            pltpu.VMEM((n_labels, 16, 128), BF16),
            pltpu.VMEM(label_shape, jnp.int32),
            dma((n_labels,)),
            dma(()),
            dma((2 * n_user * cap,)),
        ],
        50,
        nbytes=2 * blocks * half * width,
    )(own_label, own, pair_own, *far, *pair_parts, item_factors, pair_factors)

    block_flops = 4 * half * blocks * width * rank
    block_bytes = blocks * width * (half + rank) * 2
    share = rank // n_item
    payload_shape = shape((n_item, share, 128), F32)
    image_out = (shape((half, rank), BF16), VMEM)
    for number in range(ITERS):
        whole = exchange(spread).reshape(half, rank)
        if number == ITERS - 1:
            break
        if number == 0:
            late, whole, labels = lax.optimization_barrier((late, whole, labels))
            pair_late = to_pair(late)
            image, plays, reg = call(
                functools.partial(first_kernel, n_items, cap - sizes[-1]),
                [SMEM] + [VMEM] * 2 + [HBM] * 2 + [VMEM],
                [image_out, (pltpu.VMEM(plays_shape, BF16), VMEM), (shape((half, 128), F32), VMEM)],
                [
                    pltpu.VMEM((half, 128), F32),
                    pltpu.VMEM((half, rank), F32),
                    pltpu.VMEM((2, *part_shapes[-1]), BF16),
                    dma((2,)),
                ],
                20,
                flops=block_flops,
                nbytes=2 * block_bytes,
            )(labels, whole, placed, late, pair_late, factors)
        else:
            (image,) = call(
                mid_kernel,
                [VMEM] * 4,
                [image_out],
                [pltpu.VMEM((half, rank), F32)],
                12,
                flops=block_flops,
                nbytes=block_bytes,
            )(whole, reg, plays, factors)
        got = exchange(image.reshape(n_chunk, chunk, rank))
        ends = number == ITERS - 2
        outs = [(payload_shape, VMEM)] if ends else [(shape((chunk, rank), F32), VMEM)] * 3
        spread, *outs = call(
            functools.partial(vector_kernel, number),
            [VMEM] * 4,
            [(shape((n_chunk, chunk, rank), BF16), VMEM)] + outs,
            [],
            4,
        )(got, direction, residual, folded)
        if ends:
            (base,) = outs
        else:
            direction, residual, folded = outs

    (payload,) = call(
        last_kernel,
        [VMEM] * 5,
        [(payload_shape, VMEM)],
        [pltpu.VMEM((half, 128), F32), pltpu.VMEM((share, 128), F32)],
        12,
        flops=block_flops // 2,
        nbytes=block_bytes,
    )(whole, reg, base, plays, factors)
    got = lax.all_to_all(payload, "item", 0, 0, tiled=True)
    (out,) = call(final_kernel, [VMEM], [(shape((share, HALVES * half), F32), VMEM)], [], 4)(got)
    return out.T


def solution(mesh):
    placed = (
        P("item", "user", None, None),
        P("item", "user"),
        P("item", "user"),
        P("item", "user"),
        P("item", "user"),
        P("item", None),
    )
    return jax.shard_map(
        shards, mesh=mesh, in_specs=placed, out_specs=P("user", "item"), check_vma=False
    )
```

```python
import functools

import jax
import jax.numpy as jnp
from jax import lax
from jax.experimental import pallas as pl
from jax.experimental.pallas import tpu as pltpu
from jax.sharding import PartitionSpec as P

GROUPS = 8
CBLK = 4
ITERS = 4

EPS = 1.0
GUARD = 1e-06

HALVES = 2
HG = GROUPS // HALVES

BF16 = jnp.bfloat16
F32 = jnp.float32
VMEM = pl.BlockSpec(memory_space=pltpu.VMEM)
SMEM = pl.BlockSpec(memory_space=pltpu.SMEM)
HBM = pl.BlockSpec(memory_space=pltpu.HBM)


def log_tile(counts, rows, cols):
    height, width = counts.shape
    in_rows = (lax.broadcasted_iota(jnp.int32, (height, 1), 0) < rows).astype(F32)
    in_cols = (lax.broadcasted_iota(jnp.int32, (1, width), 1) < cols).astype(F32)
    return jnp.log(1.0 + counts.astype(F32) / EPS * in_cols * in_rows).astype(BF16)


def start_tiles(n_user, cap, own, owner, cell, counts, label, slots, fill, buf, sems):
    total = label.shape[0]
    for s in range(total):
        label[s] = -1
        slots[s] = -1
    for s in range(n_user):
        fill[s] = 0
    me = lax.axis_index("user")

    def visit(t, carry):
        shift = lax.rem(owner[t] - me + n_user, n_user)

        @pl.when((shift == 0) if own else (shift != 0))
        def _():
            base = 0 if own else shift - 1
            k = fill[base]
            slot = base * cap + k
            fill[base] = k + 1
            slots[slot] = t
            label[slot] = cell[t]
            pltpu.make_async_copy(counts.at[t], buf.at[slot], sems.at[slot]).start()

        return carry

    lax.fori_loop(0, counts.shape[0], visit, 0)


def label_rows(label, base, count):
    lane = lax.broadcasted_iota(jnp.int32, (16, 128), 1)
    block = jnp.zeros((16, 128), F32)
    for k in range(count):
        block = jnp.where(lane == k, label[base + k].astype(F32), block)
    return block.astype(BF16)


def pack_kernel(n_user, cap, sizes, owner, cell, rows, cols, counts, *refs):
    parts, (label, slots, fill, buf, logs, cells, sems, out_sems, cell_sems) = refs[: len(sizes)], refs[len(sizes) :]
    start_tiles(n_user, cap, False, owner, cell, counts, label, slots, fill, buf, sems)
    height = counts.shape[1]

    def cells_copy(shift):
        tail = pl.ds(sizes[0] * height, 16)
        return pltpu.make_async_copy(cells.at[shift], parts[0].at[shift, tail, :], cell_sems.at[shift])

    cells[...] = jnp.zeros_like(cells)
    for shift in range(n_user - 1):
        cells[shift, :, 0:128] = label_rows(label, shift * cap, cap)
        cells_copy(shift).start()

    def each(s, act):
        k, shift = lax.rem(s, cap), s // cap
        low = 0
        for part, size in zip(parts, sizes):

            @pl.when((slots[s] >= 0) & (k >= low) & (k < low + size))
            def _(part=part, low=low):
                row = pl.multiple_of((k - low) * height, 16)
                act(pltpu.make_async_copy(logs.at[s], part.at[shift, pl.ds(row, height), :], out_sems.at[s]))

            low += size

    def work(s, carry):
        t = slots[s]

        @pl.when(t >= 0)
        def _():
            pltpu.make_async_copy(counts.at[t], buf.at[s], sems.at[s]).wait()
            logs[s] = log_tile(buf[s], rows[t], cols[t])

        each(s, lambda copy: copy.start())
        return carry

    def finish(s, carry):
        each(s, lambda copy: copy.wait())
        return carry

    lax.fori_loop(0, label.shape[0], work, 0)
    lax.fori_loop(0, label.shape[0], finish, 0)
    for shift in range(n_user - 1):
        cells_copy(shift).wait()


def this_half():
    return lax.rem(lax.axis_index("item"), HALVES)


def rhs_kernel(n_user, cap, sizes, owner, cell, rows, cols, out_label, counts, *refs):
    n = len(sizes)
    parts, (factors, keep, send, tiles, label), bufs = refs[:n], refs[n : n + 5], refs[n + 5 : n + 5 + n]
    slots, fill, buf, logs, dense, items, sems, out_sems, part_sems, item_sem = refs[n + 5 + n :]
    start_tiles(n_user, cap, True, owner, cell, counts, label, slots, fill, buf, sems)
    height, width = counts.shape[1], counts.shape[2]
    half = HG * height
    core = this_half()
    moves = [
        pltpu.make_async_copy(part.at[:, pl.ds(0, size * height), :], target, part_sems.at[i])
        for i, (part, target, size) in enumerate(zip(parts, bufs, sizes))
    ]
    for move in moves:
        move.start()
    item_copy = pltpu.make_async_copy(factors, items, item_sem)
    item_copy.start()
    dense[...] = jnp.zeros_like(dense)

    def put(tile, shift, where):
        group, block = where // CBLK, where % CBLK
        side = jnp.where(group // HG == core, 0, 1)
        row = side * (n_user * half) + shift * half + (group % HG) * height
        one, none = jnp.ones((), BF16), jnp.zeros((), BF16)
        weighted = jnp.where(tile > none, tile + one, none)
        dense[pl.ds(pl.multiple_of(row, 16), height), pl.ds(pl.multiple_of(block * width, 128), width)] = weighted

    low = 0
    for move, source, size in zip(moves, bufs, sizes):
        move.wait()

        def put_sent(s, carry, source=source, size=size, low=low):
            shift, k = s // size, lax.rem(s, size)
            where = out_label[shift * cap + low + k]

            @pl.when(where >= 0)
            def _():
                put(source[shift, pl.ds(pl.multiple_of(k * height, 16), height), :], shift + 1, where)

            return carry

        lax.fori_loop(0, (n_user - 1) * size, put_sent, 0)
        low += size

    def own_copy(s):
        at = pl.ds(pl.multiple_of(s * height, 16), height)
        return pltpu.make_async_copy(logs.at[at], tiles.at[at], out_sems.at[s])

    tail = pl.ds(cap * height, 16)
    tail_copy = pltpu.make_async_copy(logs.at[tail], tiles.at[tail], out_sems.at[cap])
    logs[cap * height :, :] = jnp.zeros((16, width), BF16)
    logs[cap * height :, 0:128] = label_rows(label, 0, cap)
    tail_copy.start()

    def work_own(s, carry):
        t = slots[s]

        @pl.when(t >= 0)
        def _():
            pltpu.make_async_copy(counts.at[t], buf.at[s], sems.at[s]).wait()
            tile = log_tile(buf[s], rows[t], cols[t])
            logs[pl.ds(pl.multiple_of(s * height, 16), height), :] = tile
            own_copy(s).start()
            put(tile, 0, label[s])

        return carry

    def finish_own(s, carry):
        @pl.when(slots[s] >= 0)
        def _():
            own_copy(s).wait()

        return carry

    lax.fori_loop(0, cap, work_own, 0)
    item_copy.wait()
    n_chunk = keep.shape[0]
    chunk = half // n_chunk
    for side, target in ((1, send), (0, keep)):

        def dots(s, carry, side=side, target=target):
            row = pl.multiple_of((side * n_user + s) * half, 16)
            part = jnp.dot(dense[pl.ds(row, half), :], items[...], preferred_element_type=F32)
            at = pl.ds(pl.multiple_of(s * chunk, 8), chunk)
            for k in range(n_chunk):
                target[k, at, :] = part[k * chunk : (k + 1) * chunk, :].astype(target.dtype)
            return carry

        lax.fori_loop(0, n_user, dots, 0)
    lax.fori_loop(0, cap, finish_own, 0)
    tail_copy.wait()


def place_tiles(act, source, label_of, count, plays, sems, base):
    height = plays.shape[1] // HG
    core = this_half()

    def visit(k, carry):
        where = label_of(k)

        @pl.when((where >= core * (HG * CBLK)) & (where < (core + 1) * (HG * CBLK)))
        def _():
            local = where - core * (HG * CBLK)
            target = plays.at[lax.rem(local, CBLK), pl.ds(pl.multiple_of(local // CBLK * height, 16), height), :]
            tile = source.at[pl.ds(pl.multiple_of(k * height, 16), height), :]
            act(pltpu.make_async_copy(tile, target, sems.at[base + k]))

        return carry

    lax.fori_loop(0, count, visit, 0)


def place_kernel(cap, sizes, own_label, tiles, pair_tiles, *refs):
    n = len(sizes) - 1
    parts, pair_parts = refs[:n], refs[n : 2 * n]
    factors, pair_factors, plays, pair_plays, stacked, labels, raw, whole, raw_sems, label_sem, sems = refs[2 * n :]
    height = plays.shape[1] // HG
    senders = parts[0].shape[0]
    tails = [pair_tiles.at[pl.ds(cap * height, 16), pl.ds(0, 128)]]
    for first in (parts[0], pair_parts[0]):
        for s in range(senders):
            tails.append(first.at[s, pl.ds(sizes[0] * height, 16), pl.ds(0, 128)])
    reads = [pltpu.make_async_copy(tail, raw.at[i], raw_sems.at[i]) for i, tail in enumerate(tails)]
    for read in reads:
        read.start()
    plays[...] = jnp.zeros_like(plays)
    pair_plays[...] = jnp.zeros_like(pair_plays)

    def own(act):
        place_tiles(act, tiles, lambda k: own_label[k], cap, plays, sems, 0)

    def others(act):
        place_tiles(act, pair_tiles, lambda k: labels[0, k], cap, pair_plays, sems, cap)
        base = 2 * cap
        for side, group in enumerate((parts, pair_parts)):
            for s in range(senders):
                row = 1 + side * senders + s
                low = 0
                for part, size in zip(group, sizes):
                    label_of = lambda k, row=row, low=low: labels[row, low + k]
                    place_tiles(act, part.at[s], label_of, size, (plays, pair_plays)[side], sems, base)
                    low += size
                    base += size

    own(lambda copy: copy.start())
    for i, read in enumerate(reads):
        read.wait()
        whole[i : i + 1, :] = raw[i].astype(F32)[0:1, :].astype(jnp.int32)
    to_scalars = pltpu.make_async_copy(whole, labels, label_sem)
    to_scalars.start()
    items = factors.shape[0]
    stacked[:items, :] = factors[...]
    stacked[items:, :] = pair_factors[...]
    to_scalars.wait()
    others(lambda copy: copy.start())
    own(lambda copy: copy.wait())
    others(lambda copy: copy.wait())


def start_kernel(*refs):
    *parts, direction, spread = refs
    rhs = sum(p[...] for p in parts)
    direction[...] = rhs
    low = rhs.astype(BF16)
    for k in range(spread.shape[0]):
        spread[k] = low


def scaled_block(direction, factors, plays):
    projected = lax.dot_general(direction, factors, (((1,), (1,)), ((), ())), preferred_element_type=F32)
    confidence = 1.0 + plays
    return projected, (confidence * projected).astype(BF16)


def lanes(x):
    return sum(x[:, k * 128 : (k + 1) * 128] for k in range(x.shape[1] // 128))


def first_kernel(n_items, offset, side, labels, direction, placed, late, factors, *refs):
    before, after = refs[: 2 * side], refs[2 * side :]
    if side:
        image, plays, reg, acc, seen, buf, sem = after
    else:
        plays, acc, seen, buf, sem = after
    blocks, _, width = plays.shape
    senders, height = late.shape[0], plays.shape[1] // HG
    size = late.shape[1] // height
    move = pltpu.make_async_copy(late, buf, sem)
    move.start()
    plays[...] = placed[...]
    core = this_half()
    move.wait()

    def visit(i, carry):
        s, k = i // size, lax.rem(i, size)
        local = labels[1 + side * senders + s, offset + k] - core * (HG * CBLK)

        @pl.when((local >= 0) & (local < HG * CBLK))
        def _():
            row = pl.ds(pl.multiple_of(local // CBLK * height, 16), height)
            plays[lax.rem(local, CBLK), row, :] = buf[s, pl.ds(pl.multiple_of(k * height, 16), height), :]

        return carry

    lax.fori_loop(0, senders * size, visit, 0)
    for j in range(blocks):
        at = (side * blocks + j) * width
        block = factors[at : at + width, :]
        value = plays[j].astype(F32)
        _, scaled = scaled_block(direction[...], block, value)
        part = jnp.dot(scaled, block, preferred_element_type=F32)
        count = lanes(jnp.where(value > 0, 1.0, 0.0))
        if j == 0:
            acc[...] = before[0][...] + part if side else part
            seen[...] = before[1][...] + count if side else count
        else:
            acc[...] += part
            seen[...] += count
    if side:
        share = jnp.sum(seen[...], axis=1, keepdims=True) / n_items
        reg[...] = jnp.broadcast_to(share, reg.shape)
        image[...] = (acc[...] + share * direction[...].astype(F32)).astype(BF16)


def mid_kernel(direction, reg, plays, pair_plays, factors, image, acc):
    width = plays.shape[2]
    for j in range(2 * CBLK):
        block = factors[j * width : (j + 1) * width, :]
        _, scaled = scaled_block(direction[...], block, (plays, pair_plays)[j // CBLK][j % CBLK].astype(F32))
        part = jnp.dot(scaled, block, preferred_element_type=F32)
        if j == 0:
            acc[...] = part
        else:
            acc[...] += part
    image[...] = (acc[...] + reg[:, :1] * direction[...].astype(F32)).astype(BF16)


def last_kernel(direction, reg, base, plays, pair_plays, factors, payload, acc, laid):
    width = plays.shape[2]
    for j in range(2 * CBLK):
        block = factors[j * width : (j + 1) * width, :]
        projected, scaled = scaled_block(direction[...], block, (plays, pair_plays)[j // CBLK][j % CBLK].astype(F32))
        part = lanes(scaled.astype(F32) * projected)
        if j == 0:
            acc[...] = part
        else:
            acc[...] += part
    wide = direction[...].astype(F32)
    along = acc[...] + reg[:, :1] * lanes(wide * wide)
    along = jnp.broadcast_to(jnp.sum(along, axis=1, keepdims=True), acc.shape)
    laid[...] = jnp.zeros_like(laid)
    n_item = base.shape[0]
    first, free = free_lanes(acc.shape[0] * HALVES // n_item)
    put_row(laid, 0, as_row(along), first, free)
    for i in range(n_item):
        payload[i] = base[i] + laid[...]


def free_lanes(chunk):
    return 2 * chunk, 128 - 2 * chunk


def as_row(column):
    n = column.shape[0]
    return jnp.concatenate([column[k : min(k + 128, n), :].T[0:1, :] for k in range(0, n, 128)], axis=1)


def put_row(target, row, values, first, free):
    n = values.shape[1]
    for k in range(0, n, free):
        m = min(free, n - k)
        target[row + k // free : row + k // free + 1, first : first + m] = values[:, k : k + m]


def get_row(source, row, n, first, free):
    pieces = [source[row + k // free : row + k // free + 1, first : first + min(free, n - k)] for k in range(0, n, free)]
    return jnp.concatenate(pieces, axis=1)


def lay_base(folded, direction, residual, base):
    n_item, share, _ = base.shape
    chunk = folded.shape[0]
    first, free = free_lanes(chunk)
    base[...] = jnp.zeros_like(base)
    norm = jnp.sum(residual * residual, axis=1, keepdims=True)
    norm = as_row(jnp.broadcast_to(norm, (chunk, 128)))
    sides = (folded.T, direction.T)
    row = n_item // HALVES * chunk // free
    for i in range(n_item):
        for k in range(2):
            base[i, :, k * chunk : (k + 1) * chunk] = sides[k][i * share : (i + 1) * share, :]
        put_row(base.at[i], row, norm, first, free)


def final_kernel(got, out):
    n_item = got.shape[0]
    n_chunk = n_item // HALVES
    half = out.shape[1] // HALVES
    chunk = half // n_chunk
    first, free = free_lanes(chunk)
    for h in range(HALVES):
        sources = [got[k * HALVES + h] for k in range(n_chunk)]
        along = get_row(sum(sources), 0, half, first, free)
        norm = jnp.concatenate([get_row(x, half // free, chunk, first, free) for x in sources], axis=1)
        alpha = norm / (along + GUARD)
        for k, x in enumerate(sources):
            at = slice(k * chunk, (k + 1) * chunk)
            out[:, h * half + k * chunk : h * half + (k + 1) * chunk] = x[:, :chunk] + alpha[:, at] * x[:, chunk : 2 * chunk]


def vector_kernel(number, got, direction, residual, folded, spread, *outs):
    image = sum(got[k].astype(F32) for k in range(got.shape[0]))
    d, r = direction[...], residual[...]
    norm = jnp.sum(r * r, axis=1, keepdims=True)
    alpha = norm / (jnp.sum(d * image, axis=1, keepdims=True) + GUARD)
    step = alpha * d
    total = folded[...] + step if number else step
    r = r - alpha * image
    fresh = jnp.sum(r * r, axis=1, keepdims=True)
    d = r + fresh / (norm + GUARD) * d
    low = d.astype(BF16)
    for k in range(spread.shape[0]):
        spread[k] = low
    if len(outs) == 1:
        lay_base(total, d, r, outs[0])
    else:
        outs[0][...], outs[1][...], outs[2][...] = d, r, total


def shards(play_counts, tile_owner, tile_cell, tile_rows, tile_cols, item_factors):
    counts = play_counts[0]
    tiles_dev, height, width = counts.shape
    n_user = lax.axis_size("user")
    n_item = lax.axis_size("item")
    shard_items, rank = item_factors.shape
    cap = GROUPS * CBLK // n_user
    n_out = (n_user - 1) * cap
    n_chunk = n_item // HALVES
    half = HG * height
    chunk = half // n_chunk
    n_items = float(shard_items * n_item)
    blocks = HALVES * CBLK
    pair = [(i, i ^ 1) for i in range(n_item)]
    groups = [[h + HALVES * k for k in range(n_chunk)] for h in range(HALVES)]

    def shape(dims, dtype):
        return jax.ShapeDtypeStruct(dims, dtype)

    def call(kernel, ins, outs, scratch, grant, flops=0, nbytes=0, aliases=None):
        return pl.pallas_call(
            kernel,
            out_shape=[o[0] for o in outs],
            in_specs=ins,
            out_specs=[o[1] for o in outs],
            scratch_shapes=scratch,
            input_output_aliases=aliases or {},
            compiler_params=pltpu.CompilerParams(vmem_limit_bytes=grant * 2**20),
            cost_estimate=pl.CostEstimate(flops=flops, bytes_accessed=nbytes, transcendentals=0),
        )

    def over_users(x, shift):
        return lax.ppermute(x, "user", [(u, (u + shift) % n_user) for u in range(n_user)])

    def from_users(x):
        got = [over_users(x[s - 1 : s], s) for s in range(1, n_user)]
        return jnp.concatenate(got) if n_user > 2 else got[0]

    def to_pair(x):
        return lax.ppermute(x, "item", pair)

    def exchange(x):
        return lax.all_to_all(x, "item", 0, 0, axis_index_groups=groups, tiled=True)

    route = (tile_owner[0], tile_cell[0], tile_rows[0], tile_cols[0])
    dma = pltpu.SemaphoreType.DMA
    sizes = [cap - cap // 4, cap // 4]
    part_shapes = [(n_user - 1, size * height, width) for size in sizes]
    sent_shapes = [(n_user - 1, size * height + (0 if i else 16), width) for i, size in enumerate(sizes)]
    *parts, out_label = call(
        functools.partial(pack_kernel, n_user, cap, sizes),
        [SMEM] * 4 + [HBM],
        [(shape(sent, BF16), HBM) for sent in sent_shapes] + [(shape((n_out,), jnp.int32), SMEM)],
        [
            pltpu.SMEM((n_out,), jnp.int32),
            pltpu.SMEM((n_user,), jnp.int32),
            pltpu.VMEM((n_out, height, width), jnp.int32),
            pltpu.VMEM((n_out, height, width), BF16),
            pltpu.VMEM((n_user - 1, 16, width), BF16),
            dma((n_out,)),
            dma((n_out,)),
            dma((n_user - 1,)),
        ],
        56,
        nbytes=n_out * height * width * 6,
    )(*route, counts)
    far = [from_users(part) for part in parts[:-1]]
    pair_factors = to_pair(item_factors)

    state = (n_chunk, n_user * chunk, rank)
    keep, send, own, own_label = call(
        functools.partial(rhs_kernel, n_user, cap, sizes),
        [SMEM] * 5 + [HBM] * (2 + len(sizes)),
        [
            (pltpu.VMEM(state, F32), VMEM),
            (pltpu.VMEM(state, BF16), VMEM),
            (shape((cap * height + 16, width), BF16), HBM),
            (shape((cap,), jnp.int32), SMEM),
        ],
        [pltpu.VMEM(part, BF16) for part in part_shapes]
        + [
            pltpu.SMEM((cap,), jnp.int32),
            pltpu.SMEM((n_user,), jnp.int32),
            pltpu.VMEM((cap, height, width), jnp.int32),
            pltpu.VMEM((cap * height + 16, width), BF16),
            pltpu.VMEM((HALVES * n_user * half, shard_items), BF16),
            pltpu.VMEM((shard_items, rank), BF16),
            dma((cap,)),
            dma((cap + 1,)),
            dma((len(sizes),)),
            dma(()),
        ],
        56,
        flops=2 * HALVES * n_user * half * shard_items * rank,
        nbytes=2 * tiles_dev * height * width * 4,
    )(*route, out_label, counts, *parts, item_factors)

    summed = exchange((keep + to_pair(send).astype(F32)).astype(BF16))
    pair_own = to_pair(own)
    summed = jnp.sum(summed.astype(F32), axis=0).reshape(n_user, chunk, rank)
    last_part, summed = lax.optimization_barrier((parts[-1], summed))
    terms = [summed[0]] + [over_users(summed[s], s) for s in range(1, n_user)]
    direction, spread = call(
        start_kernel,
        [VMEM] * n_user,
        [(shape((chunk, rank), F32), VMEM), (shape((n_chunk, chunk, rank), BF16), VMEM)],
        [],
        4,
    )(*terms)
    residual = folded = direction
    late = from_users(last_part)
    pair_parts = [to_pair(part) for part in far]
    plays_shape = (CBLK, half, width)
    n_labels = 2 * (n_user - 1) + 1
    label_shape = (-(-n_labels // 8) * 8, 128)
    placed, pair_placed, factors, labels = call(
        functools.partial(place_kernel, cap, sizes),
        [SMEM] + [HBM] * (2 + 2 * len(far)) + [VMEM] * 2,
        [
            (shape(plays_shape, BF16), VMEM),
            (shape(plays_shape, BF16), VMEM),
            (pltpu.VMEM((HALVES * shard_items, rank), BF16), VMEM),
            (shape(label_shape, jnp.int32), SMEM),
        ],
        [
            pltpu.VMEM((n_labels, 16, 128), BF16),
            pltpu.VMEM(label_shape, jnp.int32),
            dma((n_labels,)),
            dma(()),
            dma((2 * n_user * cap,)),
        ],
        50,
        nbytes=2 * blocks * half * width,
    )(own_label, own, pair_own, *far, *pair_parts, item_factors, pair_factors)

    block_flops = 4 * half * blocks * width * rank
    block_bytes = blocks * width * (half + rank) * 2
    share = rank // n_item
    payload_shape = shape((n_item, share, 128), F32)
    image_out = (shape((half, rank), BF16), VMEM)
    for number in range(ITERS):
        whole = exchange(spread).reshape(half, rank)
        if number == ITERS - 1:
            break
        if number == 0:
            late, whole, labels = lax.optimization_barrier((late, whole, labels))
            pair_late = to_pair(late)
            acc_out, seen_out = shape((half, rank), F32), shape((half, 128), F32)
            plays_out = (pltpu.VMEM(plays_shape, BF16), VMEM)
            buffers = [pltpu.VMEM(part_shapes[-1], BF16), dma(())]
            plays, acc, seen = call(
                functools.partial(first_kernel, n_items, cap - sizes[-1], 0),
                [SMEM, VMEM, VMEM, HBM, VMEM],
                [plays_out, (acc_out, VMEM), (seen_out, VMEM)],
                buffers,
                20,
                flops=block_flops // 2,
                nbytes=block_bytes,
            )(labels, whole, placed, late, factors)
            image, pair_plays, reg = call(
                functools.partial(first_kernel, n_items, cap - sizes[-1], 1),
                [SMEM, VMEM, VMEM, HBM, VMEM, VMEM, VMEM],
                [image_out, plays_out, (seen_out, VMEM)],
                [pltpu.VMEM((half, rank), F32), pltpu.VMEM((half, 128), F32)] + buffers,
                20,
                flops=block_flops // 2,
                nbytes=block_bytes,
            )(labels, whole, pair_placed, pair_late, factors, acc, seen)
        else:
            (image,) = call(
                mid_kernel,
                [VMEM] * 5,
                [image_out],
                [pltpu.VMEM((half, rank), F32)],
                12,
                flops=block_flops,
                nbytes=block_bytes,
            )(whole, reg, plays, pair_plays, factors)
        got = exchange(image.reshape(n_chunk, chunk, rank))
        ends = number == ITERS - 2
        outs = [(payload_shape, VMEM)] if ends else [(shape((chunk, rank), F32), VMEM)] * 3
        spread, *outs = call(
            functools.partial(vector_kernel, number),
            [VMEM] * 4,
            [(shape((n_chunk, chunk, rank), BF16), VMEM)] + outs,
            [],
            4,
        )(got, direction, residual, folded)
        if ends:
            (base,) = outs
        else:
            direction, residual, folded = outs

    (payload,) = call(
        last_kernel,
        [VMEM] * 6,
        [(payload_shape, VMEM)],
        [pltpu.VMEM((half, 128), F32), pltpu.VMEM((share, 128), F32)],
        12,
        flops=block_flops // 2,
        nbytes=block_bytes,
    )(whole, reg, base, plays, pair_plays, factors)
    got = lax.all_to_all(payload, "item", 0, 0, tiled=True)
    (out,) = call(final_kernel, [VMEM], [(shape((share, HALVES * half), F32), VMEM)], [], 4)(got)
    return out.T


def solution(mesh):
    placed = (
        P("item", "user", None, None),
        P("item", "user"),
        P("item", "user"),
        P("item", "user"),
        P("item", "user"),
        P("item", None),
    )
    return jax.shard_map(
        shards, mesh=mesh, in_specs=placed, out_specs=P("user", "item"), check_vma=False
    )
```

```python
import functools

import jax
import jax.numpy as jnp
from jax import lax
from jax.experimental import pallas as pl
from jax.experimental.pallas import tpu as pltpu
from jax.sharding import PartitionSpec as P

GROUPS = 8
CBLK = 4
ITERS = 4

EPS = 1.0
GUARD = 1e-06

HALVES = 2
HG = GROUPS // HALVES

BF16 = jnp.bfloat16
F32 = jnp.float32
VMEM = pl.BlockSpec(memory_space=pltpu.VMEM)
SMEM = pl.BlockSpec(memory_space=pltpu.SMEM)
HBM = pl.BlockSpec(memory_space=pltpu.HBM)


def log_tile(counts, rows, cols):
    height, width = counts.shape
    in_rows = (lax.broadcasted_iota(jnp.int32, (height, 1), 0) < rows).astype(F32)
    in_cols = (lax.broadcasted_iota(jnp.int32, (1, width), 1) < cols).astype(F32)
    return jnp.log(1.0 + counts.astype(F32) / EPS * in_cols * in_rows).astype(BF16)


def start_tiles(n_user, cap, own, owner, cell, counts, label, slots, fill, buf, sems):
    total = label.shape[0]
    for s in range(total):
        label[s] = -1
        slots[s] = -1
    for s in range(n_user):
        fill[s] = 0
    me = lax.axis_index("user")

    def visit(t, carry):
        shift = lax.rem(owner[t] - me + n_user, n_user)

        @pl.when((shift == 0) if own else (shift != 0))
        def _():
            base = 0 if own else shift - 1
            k = fill[base]
            slot = base * cap + k
            fill[base] = k + 1
            slots[slot] = t
            label[slot] = cell[t]
            pltpu.make_async_copy(counts.at[t], buf.at[slot], sems.at[slot]).start()

        return carry

    lax.fori_loop(0, counts.shape[0], visit, 0)


def label_rows(label, base, count):
    lane = lax.broadcasted_iota(jnp.int32, (16, 128), 1)
    block = jnp.zeros((16, 128), F32)
    for k in range(count):
        block = jnp.where(lane == k, label[base + k].astype(F32), block)
    return block.astype(BF16)


def pack_kernel(n_user, cap, sizes, owner, cell, rows, cols, counts, *refs):
    parts, (label, slots, fill, buf, logs, cells, sems, out_sems, cell_sems) = refs[: len(sizes)], refs[len(sizes) :]
    start_tiles(n_user, cap, False, owner, cell, counts, label, slots, fill, buf, sems)
    height = counts.shape[1]

    def cells_copy(shift):
        tail = pl.ds(sizes[0] * height, 16)
        return pltpu.make_async_copy(cells.at[shift], parts[0].at[shift, tail, :], cell_sems.at[shift])

    cells[...] = jnp.zeros_like(cells)
    for shift in range(n_user - 1):
        cells[shift, :, 0:128] = label_rows(label, shift * cap, cap)
        cells_copy(shift).start()

    def each(s, act):
        k, shift = lax.rem(s, cap), s // cap
        low = 0
        for part, size in zip(parts, sizes):

            @pl.when((slots[s] >= 0) & (k >= low) & (k < low + size))
            def _(part=part, low=low):
                row = pl.multiple_of((k - low) * height, 16)
                act(pltpu.make_async_copy(logs.at[s], part.at[shift, pl.ds(row, height), :], out_sems.at[s]))

            low += size

    def work(s, carry):
        t = slots[s]

        @pl.when(t >= 0)
        def _():
            pltpu.make_async_copy(counts.at[t], buf.at[s], sems.at[s]).wait()
            logs[s] = log_tile(buf[s], rows[t], cols[t])

        each(s, lambda copy: copy.start())
        return carry

    def finish(s, carry):
        each(s, lambda copy: copy.wait())
        return carry

    lax.fori_loop(0, label.shape[0], work, 0)
    lax.fori_loop(0, label.shape[0], finish, 0)
    for shift in range(n_user - 1):
        cells_copy(shift).wait()


def this_half():
    return lax.rem(lax.axis_index("item"), HALVES)


def rhs_kernel(n_user, cap, sizes, owner, cell, rows, cols, out_label, counts, *refs):
    n = len(sizes)
    parts, (factors, keep, send, tiles, label), bufs = refs[:n], refs[n : n + 5], refs[n + 5 : n + 5 + n]
    slots, fill, buf, logs, dense, items, sems, out_sems, part_sems, item_sem = refs[n + 5 + n :]
    start_tiles(n_user, cap, True, owner, cell, counts, label, slots, fill, buf, sems)
    height, width = counts.shape[1], counts.shape[2]
    half = HG * height
    core = this_half()
    moves = [
        pltpu.make_async_copy(part.at[:, pl.ds(0, size * height), :], target, part_sems.at[i])
        for i, (part, target, size) in enumerate(zip(parts, bufs, sizes))
    ]
    for move in moves:
        move.start()
    item_copy = pltpu.make_async_copy(factors, items, item_sem)
    item_copy.start()
    dense[...] = jnp.zeros_like(dense)

    def put(tile, shift, where):
        group, block = where // CBLK, where % CBLK
        side = jnp.where(group // HG == core, 0, 1)
        row = side * (n_user * half) + shift * half + (group % HG) * height
        one, none = jnp.ones((), BF16), jnp.zeros((), BF16)
        weighted = jnp.where(tile > none, tile + one, none)
        dense[pl.ds(pl.multiple_of(row, 16), height), pl.ds(pl.multiple_of(block * width, 128), width)] = weighted

    low = 0
    for move, source, size in zip(moves, bufs, sizes):
        move.wait()

        def put_sent(s, carry, source=source, size=size, low=low):
            shift, k = s // size, lax.rem(s, size)
            where = out_label[shift * cap + low + k]

            @pl.when(where >= 0)
            def _():
                put(source[shift, pl.ds(pl.multiple_of(k * height, 16), height), :], shift + 1, where)

            return carry

        lax.fori_loop(0, (n_user - 1) * size, put_sent, 0)
        low += size

    def own_copy(s):
        at = pl.ds(pl.multiple_of(s * height, 16), height)
        return pltpu.make_async_copy(logs.at[at], tiles.at[at], out_sems.at[s])

    tail = pl.ds(cap * height, 16)
    tail_copy = pltpu.make_async_copy(logs.at[tail], tiles.at[tail], out_sems.at[cap])
    logs[cap * height :, :] = jnp.zeros((16, width), BF16)
    logs[cap * height :, 0:128] = label_rows(label, 0, cap)
    tail_copy.start()

    def work_own(s, carry):
        t = slots[s]

        @pl.when(t >= 0)
        def _():
            pltpu.make_async_copy(counts.at[t], buf.at[s], sems.at[s]).wait()
            tile = log_tile(buf[s], rows[t], cols[t])
            logs[pl.ds(pl.multiple_of(s * height, 16), height), :] = tile
            own_copy(s).start()
            put(tile, 0, label[s])

        return carry

    def finish_own(s, carry):
        @pl.when(slots[s] >= 0)
        def _():
            own_copy(s).wait()

        return carry

    lax.fori_loop(0, cap, work_own, 0)
    item_copy.wait()
    n_chunk = keep.shape[0]
    chunk = half // n_chunk
    for side, target in ((1, send), (0, keep)):

        def dots(s, carry, side=side, target=target):
            row = pl.multiple_of((side * n_user + s) * half, 16)
            part = jnp.dot(dense[pl.ds(row, half), :], items[...], preferred_element_type=F32)
            at = pl.ds(pl.multiple_of(s * chunk, 8), chunk)
            for k in range(n_chunk):
                target[k, at, :] = part[k * chunk : (k + 1) * chunk, :].astype(target.dtype)
            return carry

        lax.fori_loop(0, n_user, dots, 0)
    lax.fori_loop(0, cap, finish_own, 0)
    tail_copy.wait()


def place_tiles(act, source, label_of, count, plays, sems, base):
    height = plays.shape[1] // HG
    core = this_half()

    def visit(k, carry):
        where = label_of(k)

        @pl.when((where >= core * (HG * CBLK)) & (where < (core + 1) * (HG * CBLK)))
        def _():
            local = where - core * (HG * CBLK)
            target = plays.at[lax.rem(local, CBLK), pl.ds(pl.multiple_of(local // CBLK * height, 16), height), :]
            tile = source.at[pl.ds(pl.multiple_of(k * height, 16), height), :]
            act(pltpu.make_async_copy(tile, target, sems.at[base + k]))

        return carry

    lax.fori_loop(0, count, visit, 0)


def place_kernel(cap, sizes, own_label, tiles, pair_tiles, *refs):
    n = len(sizes) - 1
    parts, pair_parts = refs[:n], refs[n : 2 * n]
    factors, pair_factors, plays, pair_plays, stacked, labels, raw, whole, raw_sems, label_sem, sems = refs[2 * n :]
    height = plays.shape[1] // HG
    senders = parts[0].shape[0]
    tails = [pair_tiles.at[pl.ds(cap * height, 16), pl.ds(0, 128)]]
    for first in (parts[0], pair_parts[0]):
        for s in range(senders):
            tails.append(first.at[s, pl.ds(sizes[0] * height, 16), pl.ds(0, 128)])
    reads = [pltpu.make_async_copy(tail, raw.at[i], raw_sems.at[i]) for i, tail in enumerate(tails)]
    for read in reads:
        read.start()
    plays[...] = jnp.zeros_like(plays)
    pair_plays[...] = jnp.zeros_like(pair_plays)

    def own(act):
        place_tiles(act, tiles, lambda k: own_label[k], cap, plays, sems, 0)

    def others(act):
        place_tiles(act, pair_tiles, lambda k: labels[0, k], cap, pair_plays, sems, cap)
        base = 2 * cap
        for side, group in enumerate((parts, pair_parts)):
            for s in range(senders):
                row = 1 + side * senders + s
                low = 0
                for part, size in zip(group, sizes):
                    label_of = lambda k, row=row, low=low: labels[row, low + k]
                    place_tiles(act, part.at[s], label_of, size, (plays, pair_plays)[side], sems, base)
                    low += size
                    base += size

    own(lambda copy: copy.start())
    for i, read in enumerate(reads):
        read.wait()
        whole[i : i + 1, :] = raw[i].astype(F32)[0:1, :].astype(jnp.int32)
    to_scalars = pltpu.make_async_copy(whole, labels, label_sem)
    to_scalars.start()
    items = factors.shape[0]
    stacked[:items, :] = factors[...]
    stacked[items:, :] = pair_factors[...]
    to_scalars.wait()
    others(lambda copy: copy.start())
    own(lambda copy: copy.wait())
    others(lambda copy: copy.wait())


def start_kernel(*refs):
    *parts, direction, spread = refs
    rhs = sum(p[...] for p in parts)
    direction[...] = rhs
    low = rhs.astype(BF16)
    for k in range(spread.shape[0]):
        spread[k] = low


def scaled_block(direction, factors, plays):
    projected = lax.dot_general(direction, factors, (((1,), (1,)), ((), ())), preferred_element_type=F32)
    confidence = 1.0 + plays
    return projected, (confidence * projected).astype(BF16)


def lanes(x):
    return sum(x[:, k * 128 : (k + 1) * 128] for k in range(x.shape[1] // 128))


def first_kernel(n_items, offset, side, labels, direction, placed, late, factors, *refs):
    before, after = refs[: 2 * side], refs[2 * side :]
    if side:
        image, plays, reg, acc, seen, buf, sem = after
    else:
        plays, acc, seen, buf, sem = after
    blocks, _, width = plays.shape
    senders, height = late.shape[0], plays.shape[1] // HG
    size = late.shape[1] // height
    move = pltpu.make_async_copy(late, buf, sem)
    move.start()
    plays[...] = placed[...]
    core = this_half()
    move.wait()

    def visit(i, carry):
        s, k = i // size, lax.rem(i, size)
        local = labels[1 + side * senders + s, offset + k] - core * (HG * CBLK)

        @pl.when((local >= 0) & (local < HG * CBLK))
        def _():
            row = pl.ds(pl.multiple_of(local // CBLK * height, 16), height)
            plays[lax.rem(local, CBLK), row, :] = buf[s, pl.ds(pl.multiple_of(k * height, 16), height), :]

        return carry

    lax.fori_loop(0, senders * size, visit, 0)
    for j in range(blocks):
        at = (side * blocks + j) * width
        block = factors[at : at + width, :]
        value = plays[j].astype(F32)
        _, scaled = scaled_block(direction[...], block, value)
        part = jnp.dot(scaled, block, preferred_element_type=F32)
        count = lanes(jnp.where(value > 0, 1.0, 0.0))
        if j == 0:
            acc[...] = before[0][...] + part if side else part
            seen[...] = before[1][...] + count if side else count
        else:
            acc[...] += part
            seen[...] += count
    if side:
        share = jnp.sum(seen[...], axis=1, keepdims=True) / n_items
        reg[...] = jnp.broadcast_to(share, reg.shape)
        image[...] = (acc[...] + share * direction[...].astype(F32)).astype(BF16)


def mid_kernel(direction, reg, plays, pair_plays, factors, image, acc):
    width = plays.shape[2]
    for j in range(2 * CBLK):
        block = factors[j * width : (j + 1) * width, :]
        _, scaled = scaled_block(direction[...], block, (plays, pair_plays)[j // CBLK][j % CBLK].astype(F32))
        part = jnp.dot(scaled, block, preferred_element_type=F32)
        if j == 0:
            acc[...] = part
        else:
            acc[...] += part
    image[...] = (acc[...] + reg[:, :1] * direction[...].astype(F32)).astype(BF16)


def last_kernel(direction, reg, base, plays, pair_plays, factors, payload, acc, laid):
    width = plays.shape[2]
    for j in range(2 * CBLK):
        block = factors[j * width : (j + 1) * width, :]
        projected, scaled = scaled_block(direction[...], block, (plays, pair_plays)[j // CBLK][j % CBLK].astype(F32))
        part = lanes(scaled.astype(F32) * projected)
        if j == 0:
            acc[...] = part
        else:
            acc[...] += part
    wide = direction[...].astype(F32)
    along = acc[...] + reg[:, :1] * lanes(wide * wide)
    along = jnp.broadcast_to(jnp.sum(along, axis=1, keepdims=True), acc.shape)
    laid[...] = jnp.zeros_like(laid)
    n_item = base.shape[0]
    first, free = free_lanes(acc.shape[0] * HALVES // n_item)
    put_row(laid, 0, as_row(along), first, free)
    for i in range(n_item):
        payload[i] = base[i] + laid[...]


def free_lanes(chunk):
    return 2 * chunk, 128 - 2 * chunk


def as_row(column):
    n = column.shape[0]
    return jnp.concatenate([column[k : min(k + 128, n), :].T[0:1, :] for k in range(0, n, 128)], axis=1)


def put_row(target, row, values, first, free):
    n = values.shape[1]
    for k in range(0, n, free):
        m = min(free, n - k)
        target[row + k // free : row + k // free + 1, first : first + m] = values[:, k : k + m]


def get_row(source, row, n, first, free):
    pieces = [source[row + k // free : row + k // free + 1, first : first + min(free, n - k)] for k in range(0, n, free)]
    return jnp.concatenate(pieces, axis=1)


def lay_base(folded, direction, residual, base):
    n_item, share, _ = base.shape
    chunk = folded.shape[0]
    first, free = free_lanes(chunk)
    base[...] = jnp.zeros_like(base)
    norm = jnp.sum(residual * residual, axis=1, keepdims=True)
    norm = as_row(jnp.broadcast_to(norm, (chunk, 128)))
    sides = (folded.T, direction.T)
    row = n_item // HALVES * chunk // free
    for i in range(n_item):
        for k in range(2):
            base[i, :, k * chunk : (k + 1) * chunk] = sides[k][i * share : (i + 1) * share, :]
        put_row(base.at[i], row, norm, first, free)


def final_kernel(got, out):
    n_item = got.shape[0]
    n_chunk = n_item // HALVES
    half = out.shape[1] // HALVES
    chunk = half // n_chunk
    first, free = free_lanes(chunk)
    for h in range(HALVES):
        sources = [got[k * HALVES + h] for k in range(n_chunk)]
        along = get_row(sum(sources), 0, half, first, free)
        norm = jnp.concatenate([get_row(x, half // free, chunk, first, free) for x in sources], axis=1)
        alpha = norm / (along + GUARD)
        for k, x in enumerate(sources):
            at = slice(k * chunk, (k + 1) * chunk)
            out[:, h * half + k * chunk : h * half + (k + 1) * chunk] = x[:, :chunk] + alpha[:, at] * x[:, chunk : 2 * chunk]


def vector_kernel(number, got, direction, residual, folded, spread, *outs):
    image = sum(got[k].astype(F32) for k in range(got.shape[0]))
    d, r = direction[...], residual[...]
    norm = jnp.sum(r * r, axis=1, keepdims=True)
    alpha = norm / (jnp.sum(d * image, axis=1, keepdims=True) + GUARD)
    step = alpha * d
    total = folded[...] + step if number else step
    r = r - alpha * image
    fresh = jnp.sum(r * r, axis=1, keepdims=True)
    d = r + fresh / (norm + GUARD) * d
    low = d.astype(BF16)
    for k in range(spread.shape[0]):
        spread[k] = low
    if len(outs) == 1:
        lay_base(total, d, r, outs[0])
    else:
        outs[0][...], outs[1][...], outs[2][...] = d, r, total


def shards(play_counts, tile_owner, tile_cell, tile_rows, tile_cols, item_factors):
    counts = play_counts[0]
    tiles_dev, height, width = counts.shape
    n_user = lax.axis_size("user")
    n_item = lax.axis_size("item")
    shard_items, rank = item_factors.shape
    cap = GROUPS * CBLK // n_user
    n_out = (n_user - 1) * cap
    n_chunk = n_item // HALVES
    half = HG * height
    chunk = half // n_chunk
    n_items = float(shard_items * n_item)
    blocks = HALVES * CBLK
    pair = [(i, i ^ 1) for i in range(n_item)]
    groups = [[h + HALVES * k for k in range(n_chunk)] for h in range(HALVES)]

    def shape(dims, dtype):
        return jax.ShapeDtypeStruct(dims, dtype)

    def call(kernel, ins, outs, scratch, grant, flops=0, nbytes=0, aliases=None):
        return pl.pallas_call(
            kernel,
            out_shape=[o[0] for o in outs],
            in_specs=ins,
            out_specs=[o[1] for o in outs],
            scratch_shapes=scratch,
            input_output_aliases=aliases or {},
            compiler_params=pltpu.CompilerParams(vmem_limit_bytes=grant * 2**20),
            cost_estimate=pl.CostEstimate(flops=flops, bytes_accessed=nbytes, transcendentals=0),
        )

    def over_users(x, shift):
        return lax.ppermute(x, "user", [(u, (u + shift) % n_user) for u in range(n_user)])

    def from_users(x):
        got = [over_users(x[s - 1 : s], s) for s in range(1, n_user)]
        return jnp.concatenate(got) if n_user > 2 else got[0]

    def to_pair(x):
        return lax.ppermute(x, "item", pair)

    def exchange(x):
        return lax.all_to_all(x, "item", 0, 0, axis_index_groups=groups, tiled=True)

    route = (tile_owner[0], tile_cell[0], tile_rows[0], tile_cols[0])
    dma = pltpu.SemaphoreType.DMA
    sizes = [cap - cap // 4, cap // 4]
    part_shapes = [(n_user - 1, size * height, width) for size in sizes]
    sent_shapes = [(n_user - 1, size * height + (0 if i else 16), width) for i, size in enumerate(sizes)]
    *parts, out_label = call(
        functools.partial(pack_kernel, n_user, cap, sizes),
        [SMEM] * 4 + [HBM],
        [(shape(sent, BF16), HBM) for sent in sent_shapes] + [(shape((n_out,), jnp.int32), SMEM)],
        [
            pltpu.SMEM((n_out,), jnp.int32),
            pltpu.SMEM((n_user,), jnp.int32),
            pltpu.VMEM((n_out, height, width), jnp.int32),
            pltpu.VMEM((n_out, height, width), BF16),
            pltpu.VMEM((n_user - 1, 16, width), BF16),
            dma((n_out,)),
            dma((n_out,)),
            dma((n_user - 1,)),
        ],
        56,
        nbytes=n_out * height * width * 6,
    )(*route, counts)
    far = [from_users(part) for part in parts[:-1]]
    pair_factors = to_pair(item_factors)

    state = (n_chunk, n_user * chunk, rank)
    keep, send, own, own_label = call(
        functools.partial(rhs_kernel, n_user, cap, sizes),
        [SMEM] * 5 + [HBM] * (2 + len(sizes)),
        [
            (pltpu.VMEM(state, F32), VMEM),
            (pltpu.VMEM(state, BF16), VMEM),
            (shape((cap * height + 16, width), BF16), HBM),
            (shape((cap,), jnp.int32), SMEM),
        ],
        [pltpu.VMEM(part, BF16) for part in part_shapes]
        + [
            pltpu.SMEM((cap,), jnp.int32),
            pltpu.SMEM((n_user,), jnp.int32),
            pltpu.VMEM((cap, height, width), jnp.int32),
            pltpu.VMEM((cap * height + 16, width), BF16),
            pltpu.VMEM((HALVES * n_user * half, shard_items), BF16),
            pltpu.VMEM((shard_items, rank), BF16),
            dma((cap,)),
            dma((cap + 1,)),
            dma((len(sizes),)),
            dma(()),
        ],
        56,
        flops=2 * HALVES * n_user * half * shard_items * rank,
        nbytes=2 * tiles_dev * height * width * 4,
    )(*route, out_label, counts, *parts, item_factors)

    summed = exchange((keep + to_pair(send).astype(F32)).astype(BF16))
    pair_own = to_pair(own)
    summed = jnp.sum(summed.astype(F32), axis=0).reshape(n_user, chunk, rank)
    last_part, summed = lax.optimization_barrier((parts[-1], summed))
    terms = [summed[0]] + [over_users(summed[s], s) for s in range(1, n_user)]
    direction, spread = call(
        start_kernel,
        [VMEM] * n_user,
        [(shape((chunk, rank), F32), VMEM), (shape((n_chunk, chunk, rank), BF16), VMEM)],
        [],
        4,
    )(*terms)
    residual = folded = direction
    late = from_users(last_part)
    pair_parts = [to_pair(part) for part in far]
    plays_shape = (CBLK, half, width)
    n_labels = 2 * (n_user - 1) + 1
    label_shape = (-(-n_labels // 8) * 8, 128)
    placed, pair_placed, factors, labels = call(
        functools.partial(place_kernel, cap, sizes),
        [SMEM] + [HBM] * (2 + 2 * len(far)) + [VMEM] * 2,
        [
            (pltpu.VMEM(plays_shape, BF16), VMEM),
            (shape(plays_shape, BF16), VMEM),
            (pltpu.VMEM((HALVES * shard_items, rank), BF16), VMEM),
            (shape(label_shape, jnp.int32), SMEM),
        ],
        [
            pltpu.VMEM((n_labels, 16, 128), BF16),
            pltpu.VMEM(label_shape, jnp.int32),
            dma((n_labels,)),
            dma(()),
            dma((2 * n_user * cap,)),
        ],
        50,
        nbytes=2 * blocks * half * width,
    )(own_label, own, pair_own, *far, *pair_parts, item_factors, pair_factors)

    block_flops = 4 * half * blocks * width * rank
    block_bytes = blocks * width * (half + rank) * 2
    share = rank // n_item
    payload_shape = shape((n_item, share, 128), F32)
    image_out = (shape((half, rank), BF16), VMEM)
    for number in range(ITERS):
        whole = exchange(spread).reshape(half, rank)
        if number == ITERS - 1:
            break
        if number == 0:
            late, whole, labels = lax.optimization_barrier((late, whole, labels))
            pair_late = to_pair(late)
            acc_out, seen_out = shape((half, rank), F32), shape((half, 128), F32)
            plays_out = (pltpu.VMEM(plays_shape, BF16), VMEM)
            buffers = [pltpu.VMEM(part_shapes[-1], BF16), dma(())]
            plays, acc, seen = call(
                functools.partial(first_kernel, n_items, cap - sizes[-1], 0),
                [SMEM, VMEM, VMEM, HBM, VMEM],
                [plays_out, (acc_out, VMEM), (seen_out, VMEM)],
                buffers,
                20,
                flops=block_flops // 2,
                nbytes=block_bytes,
            )(labels, whole, placed, late, factors)
            image, pair_plays, reg = call(
                functools.partial(first_kernel, n_items, cap - sizes[-1], 1),
                [SMEM, VMEM, VMEM, HBM, VMEM, VMEM, VMEM],
                [image_out, plays_out, (seen_out, VMEM)],
                [pltpu.VMEM((half, rank), F32), pltpu.VMEM((half, 128), F32)] + buffers,
                20,
                flops=block_flops // 2,
                nbytes=block_bytes,
            )(labels, whole, pair_placed, pair_late, factors, acc, seen)
        else:
            (image,) = call(
                mid_kernel,
                [VMEM] * 5,
                [image_out],
                [pltpu.VMEM((half, rank), F32)],
                12,
                flops=block_flops,
                nbytes=block_bytes,
            )(whole, reg, plays, pair_plays, factors)
        got = exchange(image.reshape(n_chunk, chunk, rank))
        ends = number == ITERS - 2
        outs = [(payload_shape, VMEM)] if ends else [(shape((chunk, rank), F32), VMEM)] * 3
        spread, *outs = call(
            functools.partial(vector_kernel, number),
            [VMEM] * 4,
            [(shape((n_chunk, chunk, rank), BF16), VMEM)] + outs,
            [],
            4,
        )(got, direction, residual, folded)
        if ends:
            (base,) = outs
        else:
            direction, residual, folded = outs

    (payload,) = call(
        last_kernel,
        [VMEM] * 6,
        [(payload_shape, VMEM)],
        [pltpu.VMEM((half, 128), F32), pltpu.VMEM((share, 128), F32)],
        12,
        flops=block_flops // 2,
        nbytes=block_bytes,
    )(whole, reg, base, plays, pair_plays, factors)
    got = lax.all_to_all(payload, "item", 0, 0, tiled=True)
    (out,) = call(final_kernel, [VMEM], [(shape((share, HALVES * half), F32), VMEM)], [], 4)(got)
    return out.T


def solution(mesh):
    placed = (
        P("item", "user", None, None),
        P("item", "user"),
        P("item", "user"),
        P("item", "user"),
        P("item", "user"),
        P("item", None),
    )
    return jax.shard_map(
        shards, mesh=mesh, in_specs=placed, out_specs=P("user", "item"), check_vma=False
    )
```

```python
import functools

import jax
import jax.numpy as jnp
from jax import lax
from jax.experimental import pallas as pl
from jax.experimental.pallas import tpu as pltpu
from jax.sharding import PartitionSpec as P

GROUPS = 8
CBLK = 4
ITERS = 4

EPS = 1.0
GUARD = 1e-06

HALVES = 2
HG = GROUPS // HALVES

BF16 = jnp.bfloat16
F32 = jnp.float32
VMEM = pl.BlockSpec(memory_space=pltpu.VMEM)
SMEM = pl.BlockSpec(memory_space=pltpu.SMEM)
HBM = pl.BlockSpec(memory_space=pltpu.HBM)


def log_tile(counts, rows, cols):
    height, width = counts.shape
    in_rows = (lax.broadcasted_iota(jnp.int32, (height, 1), 0) < rows).astype(F32)
    in_cols = (lax.broadcasted_iota(jnp.int32, (1, width), 1) < cols).astype(F32)
    return jnp.log(1.0 + counts.astype(F32) / EPS * in_cols * in_rows).astype(BF16)


def start_tiles(n_user, cap, own, owner, cell, counts, label, slots, fill, buf, sems):
    total = label.shape[0]
    for s in range(total):
        label[s] = -1
        slots[s] = -1
    for s in range(n_user):
        fill[s] = 0
    me = lax.axis_index("user")

    def visit(t, carry):
        shift = lax.rem(owner[t] - me + n_user, n_user)

        @pl.when((shift == 0) if own else (shift != 0))
        def _():
            base = 0 if own else shift - 1
            k = fill[base]
            slot = base * cap + k
            fill[base] = k + 1
            slots[slot] = t
            label[slot] = cell[t]
            pltpu.make_async_copy(counts.at[t], buf.at[slot], sems.at[slot]).start()

        return carry

    lax.fori_loop(0, counts.shape[0], visit, 0)


def label_rows(label, base, count):
    lane = lax.broadcasted_iota(jnp.int32, (16, 128), 1)
    block = jnp.zeros((16, 128), F32)
    for k in range(count):
        block = jnp.where(lane == k, label[base + k].astype(F32), block)
    return block.astype(BF16)


def pack_kernel(n_user, cap, sizes, owner, cell, rows, cols, counts, *refs):
    parts, (label, slots, fill, buf, logs, cells, sems, out_sems, cell_sems) = refs[: len(sizes)], refs[len(sizes) :]
    start_tiles(n_user, cap, False, owner, cell, counts, label, slots, fill, buf, sems)
    height = counts.shape[1]

    def cells_copy(shift):
        tail = pl.ds(sizes[0] * height, 16)
        return pltpu.make_async_copy(cells.at[shift], parts[0].at[shift, tail, :], cell_sems.at[shift])

    cells[...] = jnp.zeros_like(cells)
    for shift in range(n_user - 1):
        cells[shift, :, 0:128] = label_rows(label, shift * cap, cap)
        cells_copy(shift).start()

    def each(s, act):
        k, shift = lax.rem(s, cap), s // cap
        low = 0
        for part, size in zip(parts, sizes):

            @pl.when((slots[s] >= 0) & (k >= low) & (k < low + size))
            def _(part=part, low=low):
                row = pl.multiple_of((k - low) * height, 16)
                act(pltpu.make_async_copy(logs.at[s], part.at[shift, pl.ds(row, height), :], out_sems.at[s]))

            low += size

    def work(s, carry):
        t = slots[s]

        @pl.when(t >= 0)
        def _():
            pltpu.make_async_copy(counts.at[t], buf.at[s], sems.at[s]).wait()
            logs[s] = log_tile(buf[s], rows[t], cols[t])

        each(s, lambda copy: copy.start())
        return carry

    def finish(s, carry):
        each(s, lambda copy: copy.wait())
        return carry

    lax.fori_loop(0, label.shape[0], work, 0)
    lax.fori_loop(0, label.shape[0], finish, 0)
    for shift in range(n_user - 1):
        cells_copy(shift).wait()


def this_half():
    return lax.rem(lax.axis_index("item"), HALVES)


def rhs_kernel(n_user, cap, sizes, owner, cell, rows, cols, out_label, counts, *refs):
    n = len(sizes)
    parts, (factors, keep, send, tiles, label), bufs = refs[:n], refs[n : n + 5], refs[n + 5 : n + 5 + n]
    slots, fill, buf, logs, dense, items, sems, out_sems, part_sems, item_sem = refs[n + 5 + n :]
    height, width = counts.shape[1], counts.shape[2]
    half = HG * height
    core = this_half()
    moves = [
        pltpu.make_async_copy(part.at[:, pl.ds(0, size * height), :], target, part_sems.at[i])
        for i, (part, target, size) in enumerate(zip(parts, bufs, sizes))
    ]
    for move in moves:
        move.start()
    start_tiles(n_user, cap, True, owner, cell, counts, label, slots, fill, buf, sems)
    item_copy = pltpu.make_async_copy(factors, items, item_sem)
    item_copy.start()
    dense[...] = jnp.zeros_like(dense)

    def put(tile, shift, where):
        group, block = where // CBLK, where % CBLK
        side = jnp.where(group // HG == core, 0, 1)
        row = side * (n_user * half) + shift * half + (group % HG) * height
        one, none = jnp.ones((), BF16), jnp.zeros((), BF16)
        weighted = jnp.where(tile > none, tile + one, none)
        dense[pl.ds(pl.multiple_of(row, 16), height), pl.ds(pl.multiple_of(block * width, 128), width)] = weighted

    low = 0
    for move, source, size in zip(moves, bufs, sizes):
        move.wait()

        def put_sent(s, carry, source=source, size=size, low=low):
            shift, k = s // size, lax.rem(s, size)
            where = out_label[shift * cap + low + k]

            @pl.when(where >= 0)
            def _():
                put(source[shift, pl.ds(pl.multiple_of(k * height, 16), height), :], shift + 1, where)

            return carry

        lax.fori_loop(0, (n_user - 1) * size, put_sent, 0)
        low += size

    def own_copy(s):
        at = pl.ds(pl.multiple_of(s * height, 16), height)
        return pltpu.make_async_copy(logs.at[at], tiles.at[at], out_sems.at[s])

    tail = pl.ds(cap * height, 16)
    tail_copy = pltpu.make_async_copy(logs.at[tail], tiles.at[tail], out_sems.at[cap])
    logs[cap * height :, :] = jnp.zeros((16, width), BF16)
    logs[cap * height :, 0:128] = label_rows(label, 0, cap)
    tail_copy.start()

    def work_own(s, carry):
        t = slots[s]

        @pl.when(t >= 0)
        def _():
            pltpu.make_async_copy(counts.at[t], buf.at[s], sems.at[s]).wait()
            tile = log_tile(buf[s], rows[t], cols[t])
            logs[pl.ds(pl.multiple_of(s * height, 16), height), :] = tile
            own_copy(s).start()
            put(tile, 0, label[s])

        return carry

    def finish_own(s, carry):
        @pl.when(slots[s] >= 0)
        def _():
            own_copy(s).wait()

        return carry

    lax.fori_loop(0, cap, work_own, 0)
    item_copy.wait()
    n_chunk = keep.shape[0]
    chunk = half // n_chunk
    for side, target in ((1, send), (0, keep)):

        def dots(s, carry, side=side, target=target):
            row = pl.multiple_of((side * n_user + s) * half, 16)
            part = jnp.dot(dense[pl.ds(row, half), :], items[...], preferred_element_type=F32)
            at = pl.ds(pl.multiple_of(s * chunk, 8), chunk)
            for k in range(n_chunk):
                target[k, at, :] = part[k * chunk : (k + 1) * chunk, :].astype(target.dtype)
            return carry

        lax.fori_loop(0, n_user, dots, 0)
    lax.fori_loop(0, cap, finish_own, 0)
    tail_copy.wait()


def place_tiles(act, source, label_of, count, plays, sems, base):
    height = plays.shape[1] // HG
    core = this_half()

    def visit(k, carry):
        where = label_of(k)

        @pl.when((where >= core * (HG * CBLK)) & (where < (core + 1) * (HG * CBLK)))
        def _():
            local = where - core * (HG * CBLK)
            target = plays.at[lax.rem(local, CBLK), pl.ds(pl.multiple_of(local // CBLK * height, 16), height), :]
            tile = source.at[pl.ds(pl.multiple_of(k * height, 16), height), :]
            act(pltpu.make_async_copy(tile, target, sems.at[base + k]))

        return carry

    lax.fori_loop(0, count, visit, 0)


def place_kernel(cap, sizes, own_label, tiles, pair_tiles, *refs):
    n = len(sizes) - 1
    parts, pair_parts = refs[:n], refs[n : 2 * n]
    factors, pair_factors, plays, pair_plays, stacked, labels, raw, whole, raw_sems, label_sem, sems = refs[2 * n :]
    height = plays.shape[1] // HG
    senders = parts[0].shape[0]
    tails = [pair_tiles.at[pl.ds(cap * height, 16), pl.ds(0, 128)]]
    for first in (parts[0], pair_parts[0]):
        for s in range(senders):
            tails.append(first.at[s, pl.ds(sizes[0] * height, 16), pl.ds(0, 128)])
    reads = [pltpu.make_async_copy(tail, raw.at[i], raw_sems.at[i]) for i, tail in enumerate(tails)]
    for read in reads:
        read.start()
    plays[...] = jnp.zeros_like(plays)
    pair_plays[...] = jnp.zeros_like(pair_plays)

    def own(act):
        place_tiles(act, tiles, lambda k: own_label[k], cap, plays, sems, 0)

    def others(act):
        place_tiles(act, pair_tiles, lambda k: labels[0, k], cap, pair_plays, sems, cap)
        base = 2 * cap
        for side, group in enumerate((parts, pair_parts)):
            for s in range(senders):
                row = 1 + side * senders + s
                low = 0
                for part, size in zip(group, sizes):
                    label_of = lambda k, row=row, low=low: labels[row, low + k]
                    place_tiles(act, part.at[s], label_of, size, (plays, pair_plays)[side], sems, base)
                    low += size
                    base += size

    own(lambda copy: copy.start())
    for i, read in enumerate(reads):
        read.wait()
        whole[i : i + 1, :] = raw[i].astype(F32)[0:1, :].astype(jnp.int32)
    to_scalars = pltpu.make_async_copy(whole, labels, label_sem)
    to_scalars.start()
    items = factors.shape[0]
    stacked[:items, :] = factors[...]
    stacked[items:, :] = pair_factors[...]
    to_scalars.wait()
    others(lambda copy: copy.start())
    own(lambda copy: copy.wait())
    others(lambda copy: copy.wait())


def start_kernel(*refs):
    *parts, direction, spread = refs
    rhs = sum(p[...] for p in parts)
    direction[...] = rhs
    low = rhs.astype(BF16)
    for k in range(spread.shape[0]):
        spread[k] = low


def scaled_block(direction, factors, plays):
    projected = lax.dot_general(direction, factors, (((1,), (1,)), ((), ())), preferred_element_type=F32)
    confidence = 1.0 + plays
    return projected, (confidence * projected).astype(BF16)


def lanes(x):
    return sum(x[:, k * 128 : (k + 1) * 128] for k in range(x.shape[1] // 128))


def first_kernel(n_items, offset, side, labels, direction, placed, late, factors, *refs):
    before, after = refs[: 2 * side], refs[2 * side :]
    if side:
        image, plays, reg, acc, seen, buf, sem = after
    else:
        plays, acc, seen, buf, sem = after
    blocks, _, width = plays.shape
    senders, height = late.shape[0], plays.shape[1] // HG
    size = late.shape[1] // height
    move = pltpu.make_async_copy(late, buf, sem)
    move.start()
    plays[...] = placed[...]
    core = this_half()
    move.wait()

    def visit(i, carry):
        s, k = i // size, lax.rem(i, size)
        local = labels[1 + side * senders + s, offset + k] - core * (HG * CBLK)

        @pl.when((local >= 0) & (local < HG * CBLK))
        def _():
            row = pl.ds(pl.multiple_of(local // CBLK * height, 16), height)
            plays[lax.rem(local, CBLK), row, :] = buf[s, pl.ds(pl.multiple_of(k * height, 16), height), :]

        return carry

    lax.fori_loop(0, senders * size, visit, 0)
    for j in range(blocks):
        at = (side * blocks + j) * width
        block = factors[at : at + width, :]
        value = plays[j].astype(F32)
        _, scaled = scaled_block(direction[...], block, value)
        part = jnp.dot(scaled, block, preferred_element_type=F32)
        count = lanes(jnp.where(value > 0, 1.0, 0.0))
        if j == 0:
            acc[...] = before[0][...] + part if side else part
            seen[...] = before[1][...] + count if side else count
        else:
            acc[...] += part
            seen[...] += count
    if side:
        share = jnp.sum(seen[...], axis=1, keepdims=True) / n_items
        reg[...] = jnp.broadcast_to(share, reg.shape)
        image[...] = (acc[...] + share * direction[...].astype(F32)).astype(BF16)


def mid_kernel(direction, reg, plays, pair_plays, factors, image, acc):
    width = plays.shape[2]
    for j in range(2 * CBLK):
        block = factors[j * width : (j + 1) * width, :]
        _, scaled = scaled_block(direction[...], block, (plays, pair_plays)[j // CBLK][j % CBLK].astype(F32))
        part = jnp.dot(scaled, block, preferred_element_type=F32)
        if j == 0:
            acc[...] = part
        else:
            acc[...] += part
    image[...] = (acc[...] + reg[:, :1] * direction[...].astype(F32)).astype(BF16)


def last_kernel(direction, reg, base, plays, pair_plays, factors, payload, acc, laid):
    width = plays.shape[2]
    for j in range(2 * CBLK):
        block = factors[j * width : (j + 1) * width, :]
        projected, scaled = scaled_block(direction[...], block, (plays, pair_plays)[j // CBLK][j % CBLK].astype(F32))
        part = lanes(scaled.astype(F32) * projected)
        if j == 0:
            acc[...] = part
        else:
            acc[...] += part
    wide = direction[...].astype(F32)
    along = acc[...] + reg[:, :1] * lanes(wide * wide)
    along = jnp.broadcast_to(jnp.sum(along, axis=1, keepdims=True), acc.shape)
    laid[...] = jnp.zeros_like(laid)
    n_item = base.shape[0]
    first, free = free_lanes(acc.shape[0] * HALVES // n_item)
    put_row(laid, 0, as_row(along), first, free)
    for i in range(n_item):
        payload[i] = base[i] + laid[...]


def free_lanes(chunk):
    return 2 * chunk, 128 - 2 * chunk


def as_row(column):
    n = column.shape[0]
    return jnp.concatenate([column[k : min(k + 128, n), :].T[0:1, :] for k in range(0, n, 128)], axis=1)


def put_row(target, row, values, first, free):
    n = values.shape[1]
    for k in range(0, n, free):
        m = min(free, n - k)
        target[row + k // free : row + k // free + 1, first : first + m] = values[:, k : k + m]


def get_row(source, row, n, first, free):
    pieces = [source[row + k // free : row + k // free + 1, first : first + min(free, n - k)] for k in range(0, n, free)]
    return jnp.concatenate(pieces, axis=1)


def lay_base(folded, direction, residual, base):
    n_item, share, _ = base.shape
    chunk = folded.shape[0]
    first, free = free_lanes(chunk)
    base[...] = jnp.zeros_like(base)
    norm = jnp.sum(residual * residual, axis=1, keepdims=True)
    norm = as_row(jnp.broadcast_to(norm, (chunk, 128)))
    sides = (folded.T, direction.T)
    row = n_item // HALVES * chunk // free
    for i in range(n_item):
        for k in range(2):
            base[i, :, k * chunk : (k + 1) * chunk] = sides[k][i * share : (i + 1) * share, :]
        put_row(base.at[i], row, norm, first, free)


def final_kernel(got, out):
    n_item = got.shape[0]
    n_chunk = n_item // HALVES
    half = out.shape[1] // HALVES
    chunk = half // n_chunk
    first, free = free_lanes(chunk)
    for h in range(HALVES):
        sources = [got[k * HALVES + h] for k in range(n_chunk)]
        along = get_row(sum(sources), 0, half, first, free)
        norm = jnp.concatenate([get_row(x, half // free, chunk, first, free) for x in sources], axis=1)
        alpha = norm / (along + GUARD)
        for k, x in enumerate(sources):
            at = slice(k * chunk, (k + 1) * chunk)
            out[:, h * half + k * chunk : h * half + (k + 1) * chunk] = x[:, :chunk] + alpha[:, at] * x[:, chunk : 2 * chunk]


def vector_kernel(number, got, direction, residual, folded, spread, *outs):
    image = sum(got[k].astype(F32) for k in range(got.shape[0]))
    d, r = direction[...], residual[...]
    norm = jnp.sum(r * r, axis=1, keepdims=True)
    alpha = norm / (jnp.sum(d * image, axis=1, keepdims=True) + GUARD)
    step = alpha * d
    total = folded[...] + step if number else step
    r = r - alpha * image
    fresh = jnp.sum(r * r, axis=1, keepdims=True)
    d = r + fresh / (norm + GUARD) * d
    low = d.astype(BF16)
    for k in range(spread.shape[0]):
        spread[k] = low
    if len(outs) == 1:
        lay_base(total, d, r, outs[0])
    else:
        outs[0][...], outs[1][...], outs[2][...] = d, r, total


def shards(play_counts, tile_owner, tile_cell, tile_rows, tile_cols, item_factors):
    counts = play_counts[0]
    tiles_dev, height, width = counts.shape
    n_user = lax.axis_size("user")
    n_item = lax.axis_size("item")
    shard_items, rank = item_factors.shape
    cap = GROUPS * CBLK // n_user
    n_out = (n_user - 1) * cap
    n_chunk = n_item // HALVES
    half = HG * height
    chunk = half // n_chunk
    n_items = float(shard_items * n_item)
    blocks = HALVES * CBLK
    pair = [(i, i ^ 1) for i in range(n_item)]
    groups = [[h + HALVES * k for k in range(n_chunk)] for h in range(HALVES)]

    def shape(dims, dtype):
        return jax.ShapeDtypeStruct(dims, dtype)

    def call(kernel, ins, outs, scratch, grant, flops=0, nbytes=0, aliases=None):
        return pl.pallas_call(
            kernel,
            out_shape=[o[0] for o in outs],
            in_specs=ins,
            out_specs=[o[1] for o in outs],
            scratch_shapes=scratch,
            input_output_aliases=aliases or {},
            compiler_params=pltpu.CompilerParams(vmem_limit_bytes=grant * 2**20),
            cost_estimate=pl.CostEstimate(flops=flops, bytes_accessed=nbytes, transcendentals=0),
        )

    def over_users(x, shift):
        return lax.ppermute(x, "user", [(u, (u + shift) % n_user) for u in range(n_user)])

    def from_users(x):
        got = [over_users(x[s - 1 : s], s) for s in range(1, n_user)]
        return jnp.concatenate(got) if n_user > 2 else got[0]

    def to_pair(x):
        return lax.ppermute(x, "item", pair)

    def exchange(x):
        return lax.all_to_all(x, "item", 0, 0, axis_index_groups=groups, tiled=True)

    route = (tile_owner[0], tile_cell[0], tile_rows[0], tile_cols[0])
    dma = pltpu.SemaphoreType.DMA
    sizes = [cap - cap // 4, cap // 4]
    part_shapes = [(n_user - 1, size * height, width) for size in sizes]
    sent_shapes = [(n_user - 1, size * height + (0 if i else 16), width) for i, size in enumerate(sizes)]
    *parts, out_label = call(
        functools.partial(pack_kernel, n_user, cap, sizes),
        [SMEM] * 4 + [HBM],
        [(shape(sent, BF16), HBM) for sent in sent_shapes] + [(shape((n_out,), jnp.int32), SMEM)],
        [
            pltpu.SMEM((n_out,), jnp.int32),
            pltpu.SMEM((n_user,), jnp.int32),
            pltpu.VMEM((n_out, height, width), jnp.int32),
            pltpu.VMEM((n_out, height, width), BF16),
            pltpu.VMEM((n_user - 1, 16, width), BF16),
            dma((n_out,)),
            dma((n_out,)),
            dma((n_user - 1,)),
        ],
        56,
        nbytes=n_out * height * width * 6,
    )(*route, counts)
    far = [from_users(part) for part in parts[:-1]]
    pair_factors = to_pair(item_factors)

    state = (n_chunk, n_user * chunk, rank)
    keep, send, own, own_label = call(
        functools.partial(rhs_kernel, n_user, cap, sizes),
        [SMEM] * 5 + [HBM] * (2 + len(sizes)),
        [
            (pltpu.VMEM(state, F32), VMEM),
            (pltpu.VMEM(state, BF16), VMEM),
            (shape((cap * height + 16, width), BF16), HBM),
            (shape((cap,), jnp.int32), SMEM),
        ],
        [pltpu.VMEM(part, BF16) for part in part_shapes]
        + [
            pltpu.SMEM((cap,), jnp.int32),
            pltpu.SMEM((n_user,), jnp.int32),
            pltpu.VMEM((cap, height, width), jnp.int32),
            pltpu.VMEM((cap * height + 16, width), BF16),
            pltpu.VMEM((HALVES * n_user * half, shard_items), BF16),
            pltpu.VMEM((shard_items, rank), BF16),
            dma((cap,)),
            dma((cap + 1,)),
            dma((len(sizes),)),
            dma(()),
        ],
        56,
        flops=2 * HALVES * n_user * half * shard_items * rank,
        nbytes=2 * tiles_dev * height * width * 4,
    )(*route, out_label, counts, *parts, item_factors)

    summed = exchange((keep + to_pair(send).astype(F32)).astype(BF16))
    pair_own = to_pair(own)
    summed = jnp.sum(summed.astype(F32), axis=0).reshape(n_user, chunk, rank)
    last_part, summed = lax.optimization_barrier((parts[-1], summed))
    terms = [summed[0]] + [over_users(summed[s], s) for s in range(1, n_user)]
    direction, spread = call(
        start_kernel,
        [VMEM] * n_user,
        [(shape((chunk, rank), F32), VMEM), (shape((n_chunk, chunk, rank), BF16), VMEM)],
        [],
        4,
    )(*terms)
    residual = folded = direction
    late = from_users(last_part)
    pair_parts = [to_pair(part) for part in far]
    plays_shape = (CBLK, half, width)
    n_labels = 2 * (n_user - 1) + 1
    label_shape = (-(-n_labels // 8) * 8, 128)
    placed, pair_placed, factors, labels = call(
        functools.partial(place_kernel, cap, sizes),
        [SMEM] + [HBM] * (2 + 2 * len(far)) + [VMEM] * 2,
        [
            (pltpu.VMEM(plays_shape, BF16), VMEM),
            (shape(plays_shape, BF16), VMEM),
            (pltpu.VMEM((HALVES * shard_items, rank), BF16), VMEM),
            (shape(label_shape, jnp.int32), SMEM),
        ],
        [
            pltpu.VMEM((n_labels, 16, 128), BF16),
            pltpu.VMEM(label_shape, jnp.int32),
            dma((n_labels,)),
            dma(()),
            dma((2 * n_user * cap,)),
        ],
        50,
        nbytes=2 * blocks * half * width,
    )(own_label, own, pair_own, *far, *pair_parts, item_factors, pair_factors)

    block_flops = 4 * half * blocks * width * rank
    block_bytes = blocks * width * (half + rank) * 2
    share = rank // n_item
    payload_shape = shape((n_item, share, 128), F32)
    image_out = (shape((half, rank), BF16), VMEM)
    for number in range(ITERS):
        whole = exchange(spread).reshape(half, rank)
        if number == ITERS - 1:
            break
        if number == 0:
            late, whole, labels = lax.optimization_barrier((late, whole, labels))
            pair_late = to_pair(late)
            acc_out, seen_out = shape((half, rank), F32), shape((half, 128), F32)
            plays_out = (pltpu.VMEM(plays_shape, BF16), VMEM)
            buffers = [pltpu.VMEM(part_shapes[-1], BF16), dma(())]
            plays, acc, seen = call(
                functools.partial(first_kernel, n_items, cap - sizes[-1], 0),
                [SMEM, VMEM, VMEM, HBM, VMEM],
                [plays_out, (acc_out, VMEM), (seen_out, VMEM)],
                buffers,
                20,
                flops=block_flops // 2,
                nbytes=block_bytes,
            )(labels, whole, placed, late, factors)
            image, pair_plays, reg = call(
                functools.partial(first_kernel, n_items, cap - sizes[-1], 1),
                [SMEM, VMEM, VMEM, HBM, VMEM, VMEM, VMEM],
                [image_out, plays_out, (seen_out, VMEM)],
                [pltpu.VMEM((half, rank), F32), pltpu.VMEM((half, 128), F32)] + buffers,
                20,
                flops=block_flops // 2,
                nbytes=block_bytes,
            )(labels, whole, pair_placed, pair_late, factors, acc, seen)
        else:
            (image,) = call(
                mid_kernel,
                [VMEM] * 5,
                [image_out],
                [pltpu.VMEM((half, rank), F32)],
                12,
                flops=block_flops,
                nbytes=block_bytes,
            )(whole, reg, plays, pair_plays, factors)
        got = exchange(image.reshape(n_chunk, chunk, rank))
        ends = number == ITERS - 2
        outs = [(payload_shape, VMEM)] if ends else [(shape((chunk, rank), F32), VMEM)] * 3
        spread, *outs = call(
            functools.partial(vector_kernel, number),
            [VMEM] * 4,
            [(shape((n_chunk, chunk, rank), BF16), VMEM)] + outs,
            [],
            4,
        )(got, direction, residual, folded)
        if ends:
            (base,) = outs
        else:
            direction, residual, folded = outs

    (payload,) = call(
        last_kernel,
        [VMEM] * 6,
        [(payload_shape, VMEM)],
        [pltpu.VMEM((half, 128), F32), pltpu.VMEM((share, 128), F32)],
        12,
        flops=block_flops // 2,
        nbytes=block_bytes,
    )(whole, reg, base, plays, pair_plays, factors)
    got = lax.all_to_all(payload, "item", 0, 0, tiled=True)
    (out,) = call(final_kernel, [VMEM], [(shape((share, HALVES * half), F32), VMEM)], [], 4)(got)
    return out.T


def solution(mesh):
    placed = (
        P("item", "user", None, None),
        P("item", "user"),
        P("item", "user"),
        P("item", "user"),
        P("item", "user"),
        P("item", None),
    )
    return jax.shard_map(
        shards, mesh=mesh, in_specs=placed, out_specs=P("user", "item"), check_vma=False
    )
```
